512 devices in a mesh: rep: 32 (over y, z_lo, core), fsdp: 16 (over z_hi, x).
Axes of the slice: x: 4, y: 8, z: 8 (z_hi: 4, z_lo: 2; z = z_hi * 2 + z_lo), core: 2. Of those that a mesh axis runs over, the one named last changes fastest.
Arguments:
- tokens: bfloat16 [16384, 4096], P('rep', 'fsdp'), may hold values from -6 to 6
- gate_weight: bfloat16 [4096, 7168], P('rep', 'fsdp'), may hold values from -0.09375 to 0.09375
- up_act: bfloat16 [16384, 7168], P('rep', 'fsdp'), may hold values from -6 to 6
- cotangent: bfloat16 [16384, 7168], P('rep', 'fsdp'), may hold values from -0.099609375 to 0.099609375
Outputs:
- grad_sum: bfloat16 [4096, 7168], P('rep', 'fsdp')
- curvature: float32 [7168], P('fsdp')
- spread: float32 [7168], P('fsdp')
The draws below stay inside these ranges and needn't reach their ends.
All inputs are finite; a program needn't handle non-finite values.
Results may differ from the reference program's by a relative error of at most 0.024.
Values may be sent and summed in bfloat16 or wider, within the bound.
No kernel may reach another device: no remote copies, remote signals or barrier semaphores. Data moves between devices by JAX's collectives and lax.ppermute only.
A program may use at most 64 MiB of HBM per device.

```python
import jax
import jax.numpy as jnp
from jax import lax

D = 4096
FF = 7168
TOK = 512
REPLICAS = 32
TOKENS = 16384


def shard_levels(rng, extent, cuts, smallest, largest):
    def one(dim, shards_of):
        heights = jax.random.uniform(jax.random.fold_in(jax.random.fold_in(rng, 6), dim), (shards_of,), jnp.float32, smallest / len(cuts), largest / len(cuts))
        return jnp.repeat(jnp.exp(heights), extent[dim] // shards_of).reshape((-1,) + (1,) * (len(extent) - dim - 1))

    loudness = one(*cuts[0])
    for cut in cuts[1:]:
        loudness = loudness * one(*cut)
    return loudness


def bell_draw(own_key, extent, spread, most, pieces=(), dtype=jnp.bfloat16):
    gain = shard_levels(own_key, extent, pieces, -0.22, 0.18) if pieces else 1.0
    entries = jax.random.normal(own_key, extent, jnp.float32) * spread * gain
    return jnp.minimum(jnp.maximum(entries, -most), most).astype(dtype)


def setup_inputs(seed: int = 0) -> dict:
    splits = jax.random.split(jax.random.key(seed), 5)
    return {
        "tokens": bell_draw(splits[0], (TOKENS, D), 1.0, 6.0, ((0, 32), (1, 16))),
        "gate_weight": bell_draw(splits[1], (D, FF), D ** -0.5, 0.09375, ((0, 32), (1, 16))),
        "up_act": bell_draw(splits[2], (TOKENS, FF), 1.0, 6.0, ((0, 32), (1, 16))),
        "cotangent": bell_draw(splits[3], (TOKENS, FF), 0.015625, 0.099609375, ((0, 32), (1, 16))),
    }


def local_terms(inputs, up_rows, cot_rows, gate_weight):
    gate_pre = jnp.dot(inputs, gate_weight, preferred_element_type=jnp.float32)
    sigmoid_gate = jax.nn.sigmoid(gate_pre)
    deriv_one = sigmoid_gate * (1.0 + gate_pre * (1.0 - sigmoid_gate))
    deriv_two = sigmoid_gate * (1.0 - sigmoid_gate) * (2.0 + gate_pre * (1.0 - 2.0 * sigmoid_gate))
    weighted = cot_rows.astype(jnp.float32) * up_rows.astype(jnp.float32)
    token_coeff = (weighted * deriv_one).astype(jnp.bfloat16)
    rep_grad = lax.dot_general(inputs, token_coeff, (((0,), (0,)), ((), ())), preferred_element_type=jnp.float32).astype(jnp.bfloat16)
    return rep_grad, weighted * deriv_two


def reference(tokens, gate_weight, up_act, cotangent):
    rows_in = tokens.reshape(REPLICAS, TOK, D)
    up_in = up_act.reshape(REPLICAS, TOK, FF)
    cot_in = cotangent.reshape(REPLICAS, TOK, FF)

    def first_pass(running, blocks):
        rep_grad, unused = local_terms(blocks[0], blocks[1], blocks[2], gate_weight)
        return running + rep_grad.astype(jnp.float32), None

    grad_acc, unused = lax.scan(first_pass, jnp.zeros((D, FF), jnp.float32), (rows_in, up_in, cot_in))
    grad_sum = grad_acc.astype(jnp.bfloat16)

    def second_pass(running, blocks):
        inputs = blocks[0]
        rep_grad, bend_weight = local_terms(inputs, blocks[1], blocks[2], gate_weight)
        own_proj = jnp.dot(inputs, rep_grad, preferred_element_type=jnp.float32)
        mean_proj = jnp.dot(inputs, grad_sum, preferred_element_type=jnp.float32) / REPLICAS
        deviate = own_proj - mean_proj
        curv_part = jnp.sum(bend_weight * mean_proj * mean_proj, axis=0)
        spread_part = jnp.sum(bend_weight * deviate * deviate, axis=0)
        return (running[0] + curv_part, running[1] + spread_part), None

    zeros_row = jnp.zeros((FF,), jnp.float32)
    sums, unused = lax.scan(second_pass, (zeros_row, zeros_row), (rows_in, up_in, cot_in))
    return grad_sum, sums[0], sums[1] / (REPLICAS - 1)
```

```python
import functools

import jax
import jax.numpy as jnp
from jax import lax
from jax.experimental import pallas as pl
from jax.experimental.pallas import tpu as pltpu
from jax.sharding import Mesh
from jax.sharding import PartitionSpec as P

REP = ("y", "zl", "c")
F32, BF = jnp.float32, jnp.bfloat16
NT = (((1,), (1,)), ((), ()))
CUT = 288
VM = pl.BlockSpec(memory_space=pltpu.VMEM)
SM = pl.BlockSpec(memory_space=pltpu.SMEM)


def call(kernel, outs, operands, flops, scratch=()):
    moved = sum(a.size * a.dtype.itemsize for a in operands) + sum(
        o.size * o.dtype.itemsize for o in outs
    )
    return pl.pallas_call(
        kernel,
        out_shape=outs,
        in_specs=[SM] + [VM] * (len(operands) - 1),
        out_specs=[VM] * len(outs),
        scratch_shapes=list(scratch),
        cost_estimate=pl.CostEstimate(flops=flops, bytes_accessed=moved, transcendentals=0),
        compiler_params=pltpu.CompilerParams(vmem_limit_bytes=40 * 1024 * 1024),
    )(*operands)


def piece(tok, y, zl):
    f = 2 * y + zl
    return tok[f % 4, f // 4]


def block_of(refs, y, rel):
    if len(refs) == 4:
        return refs[rel][y], refs[2 + rel][y]
    return refs[0][y, rel], refs[1][y, rel]


def project(me, tok, refs, acc):
    mine, first = me[0], me[1] == 0
    acc[...] = jnp.zeros_like(acc)

    def step(y, unused):
        rows, cols = [], []
        for rel in (0, 1):
            own, other = block_of(refs, y, rel)
            rows += [jnp.where(first, own, other), jnp.where(first, other, own)]
            cols.append(piece(tok, y, jnp.bitwise_xor(mine, rel)))
        acc[...] += lax.dot_general(
            jnp.concatenate(rows, 1), jnp.concatenate(cols, 1), NT, preferred_element_type=F32
        )
        return unused

    lax.fori_loop(0, 8, step, 0)


def gate_kernel(me, tok, up, cot, w0, w1, w2, w3, coeff, bend, acc):
    project(me, tok, (w0, w1, w2, w3), acc)

    def part(i, unused):
        at = pl.ds(pl.multiple_of(i * 32, 32), 32)
        pre = acc[at, :]
        s = jax.nn.sigmoid(pre)
        one = s * (1.0 + pre * (1.0 - s))
        two = s * (1.0 - s) * (2.0 + pre * (1.0 - 2.0 * s))
        weighted = cot[at, :].astype(F32) * up[at, :].astype(F32)
        coeff[at, :] = (weighted * one).astype(BF)
        bend[at, :] = weighted * two
        return unused

    lax.fori_loop(0, 448 // 32, part, 0)


def grad_kernel(start, rows, me, tok, coeff, own0, own1, snd0, snd1):
    mine, first = me[0], me[1] == 0

    def step(y, unused):
        for rel, own, snd in ((0, own0, snd0), (1, own1, snd1)):
            tile = piece(tok, y, jnp.bitwise_xor(mine, rel))
            got = jnp.dot(coeff[start : start + rows, :], tile, preferred_element_type=F32)
            got = got.astype(BF)
            low, high = got[:, :128], got[:, 128:]
            own[y] = jnp.where(first, low, high)
            snd[y] = jnp.where(first, high, low)
        return unused

    lax.fori_loop(0, 8, step, 0)


def own_kernel(n, me, tok, *refs):
    project(me, tok, refs[:n], refs[n])


def mean_kernel(n, start, rows, me, tok, bend, own, *refs):
    curv, spread, acc = refs[n:]
    project(me, tok, refs[:n], acc)
    c = jnp.zeros((rows, 128), F32)
    s = jnp.zeros((rows, 128), F32)
    for k in range(4):
        lanes = slice(128 * k, 128 * k + 128)
        mean = acc[:, lanes] / 32.0
        b = bend[start : start + rows, lanes]
        off = own[:, lanes] - mean
        c += b * mean * mean
        s += b * off * off
    curv[...] = jnp.sum(c.T, axis=0, keepdims=True)
    spread[...] = jnp.sum(s.T, axis=0, keepdims=True)


def swap(value, axis):
    return lax.ppermute(value, axis, ((0, 1), (1, 0)))


def to_all(value, axis):
    count = lax.axis_size(axis)
    return lax.all_to_all(
        jnp.broadcast_to(value[None], (count, *value.shape)), axis, 0, 0, tiled=True
    )


def total(*values):
    return functools.reduce(jnp.add, [v.astype(F32) for v in values])


def shape(*lengths, dtype=BF):
    return jax.ShapeDtypeStruct(lengths, dtype)


def grads(me, tok, coeff, start, rows):
    return call(
        functools.partial(grad_kernel, start, rows),
        [shape(8, rows, 128)] * 4,
        (me, tok, coeff),
        2 * rows * 512 * 4096,
    )


def projected(me, tok, refs, rows):
    return call(
        functools.partial(own_kernel, len(refs)),
        [shape(rows, 512, dtype=F32)],
        (me, tok, *refs),
        2 * rows * 512 * 4096,
    )[0]


def terms(me, tok, bend, own, refs, start, rows):
    return call(
        functools.partial(mean_kernel, len(refs), start, rows),
        [shape(1, rows, dtype=F32)] * 2,
        (me, tok, bend, own, *refs),
        2 * rows * 512 * 4096,
        [pltpu.VMEM((rows, 512), F32)],
    )


def shards(tokens, gate_weight, up_act, cotangent):
    me = jnp.stack([lax.axis_index("zl"), lax.axis_index("c")]).astype(jnp.int32)
    tok = to_all(to_all(tokens, "zh"), "x")
    w0 = lax.all_gather(gate_weight.T, "y", axis=0)
    w1 = swap(w0, "zl")
    w2, w3 = swap(w0, "c"), swap(w1, "c")
    coeff, bend = call(
        gate_kernel,
        [shape(448, 512), shape(448, 512, dtype=F32)],
        (me, tok, up_act.T, cotangent.T, w0, w1, w2, w3),
        2 * 448 * 512 * 4096,
        [pltpu.VMEM((448, 512), F32)],
    )
    b0, b1, p0, p1 = grads(me, tok, coeff, CUT, 448 - CUT)
    sums_b = jnp.stack(
        [total(b0, swap(p0, "c")).astype(BF), total(b1, swap(p1, "c")).astype(BF)], axis=1
    )
    across_b = lax.all_to_all(sums_b, "y", 0, 0, tiled=True)
    a0, a1, q0, q1 = grads(me, tok, coeff, 0, CUT)
    sent = swap(total(a1, swap(q1, "c")).astype(BF), "zl")
    sums_a = total(a0, swap(q0, "c"), sent).astype(BF)
    own_b = projected(me, tok, (b0, b1, p0, p1), 448 - CUT)
    own_a = projected(me, tok, (a0, a1, q0, q1), CUT)
    part_b = jnp.sum(across_b.astype(F32), axis=0)
    grad_b = total(part_b[0], swap(part_b[1].astype(BF), "zl")).astype(BF)
    across_a = lax.all_to_all(sums_a, "y", 0, 0, tiled=True)
    grad_a = jnp.sum(across_a.astype(F32), axis=0).astype(BF)
    u0 = to_all(grad_a, "y")
    u1 = swap(u0, "zl")
    v0 = to_all(jnp.stack([grad_b, swap(grad_b, "zl")]), "y")
    u2, u3 = swap(u0, "c"), swap(u1, "c")
    v1 = swap(v0, "c")
    curv_a, spread_a = terms(me, tok, bend, own_a, (u0, u1, u2, u3), 0, CUT)
    curv_b, spread_b = terms(me, tok, bend, own_b, (v0, v1), CUT, 448 - CUT)
    line = jnp.concatenate([curv_a, curv_b, spread_a, spread_b], axis=1)
    whole = jnp.sum(to_all(line, REP), axis=(0, 1))
    grad = jnp.concatenate([grad_a, grad_b], axis=0).T
    return grad, whole[:448], whole[448:] / 31


def solution(mesh):
    torus = Mesh(mesh.devices.reshape(8, 2, 2, 4, 4), ("y", "zl", "c", "zh", "x"))
    fsdp = ("zh", "x")
    return jax.shard_map(
        shards,
        mesh=torus,
        in_specs=(P(REP, fsdp),) * 4,
        out_specs=(P(REP, fsdp), P(fsdp), P(fsdp)),
        check_vma=False,
    )
```

```python
import functools

import jax
import jax.numpy as jnp
from jax import lax
from jax.experimental import pallas as pl
from jax.experimental.pallas import tpu as pltpu
from jax.sharding import Mesh
from jax.sharding import PartitionSpec as P

REP = ("y", "zl", "c")
F32, BF = jnp.float32, jnp.bfloat16
NT = (((1,), (1,)), ((), ()))
CUT = 336
VM = pl.BlockSpec(memory_space=pltpu.VMEM)
SM = pl.BlockSpec(memory_space=pltpu.SMEM)


def call(kernel, outs, operands, flops, scratch=()):
    moved = sum(a.size * a.dtype.itemsize for a in operands) + sum(
        o.size * o.dtype.itemsize for o in outs
    )
    return pl.pallas_call(
        kernel,
        out_shape=outs,
        in_specs=[SM] + [VM] * (len(operands) - 1),
        out_specs=[VM] * len(outs),
        scratch_shapes=list(scratch),
        cost_estimate=pl.CostEstimate(flops=flops, bytes_accessed=moved, transcendentals=0),
        compiler_params=pltpu.CompilerParams(vmem_limit_bytes=24 * 1024 * 1024),
    )(*operands)


def block_of(refs, y, rel):
    a0, a1, a2, a3, b0, b1 = refs
    own, other = ((a0, a2), (a1, a3))[rel]
    return (
        jnp.concatenate([own[y], b0[y, rel]], 0),
        jnp.concatenate([other[y], b1[y, rel]], 0),
    )


def project(me, tok, block, acc):
    mine, first = me[0], me[1] == 0
    acc[...] = jnp.zeros_like(acc)

    def step(y, unused):
        rows, cols = [], []
        for rel in (0, 1):
            own, other = block(y, rel)
            rows += [jnp.where(first, own, other), jnp.where(first, other, own)]
            cols.append(tok[2 * y + jnp.bitwise_xor(mine, rel)])
        acc[...] += lax.dot_general(
            jnp.concatenate(rows, 1), jnp.concatenate(cols, 1), NT, preferred_element_type=F32
        )
        return unused

    lax.fori_loop(0, 8, step, 0)


def gate_kernel(me, t0, t1, t3, t2a, t2b, up, cot, w0, w1, w2, w3, tok, coeff, bend, acc):
    for d in range(4):
        x = lax.rem(me[2] + d, 4)
        for z in range(4):
            tok[4 * z + x] = (t0[z], t1[z], (t2a, t2b)[z // 2][z % 2], t3[z])[d]
    project(me, tok, lambda y, rel: ((w0[y], w2[y]), (w1[y], w3[y]))[rel], acc)

    def part(i, unused):
        at = pl.ds(pl.multiple_of(i * 32, 32), 32)
        pre = acc[at, :]
        s = jax.nn.sigmoid(pre)
        one = s * (1.0 + pre * (1.0 - s))
        two = s * (1.0 - s) * (2.0 + pre * (1.0 - 2.0 * s))
        weighted = cot[at, :].astype(F32) * up[at, :].astype(F32)
        coeff[at, :] = (weighted * one).astype(BF)
        bend[at, :] = weighted * two
        return unused

    lax.fori_loop(0, 448 // 32, part, 0)


def grad_kernel(me, tok, coeff, own0, own1, sent, own_b, sent_b):
    mine, first = me[0], me[1] == 0

    def step(y, unused):
        for rel, own in ((0, own0), (1, own1)):
            tile = tok[2 * y + jnp.bitwise_xor(mine, rel)]
            got = jnp.dot(coeff[...], tile, preferred_element_type=F32).astype(BF)
            low, high = got[:, :128], got[:, 128:]
            keep, give = jnp.where(first, low, high), jnp.where(first, high, low)
            own[y] = keep[:CUT]
            own_b[y, rel] = keep[CUT:]
            sent[rel, y] = give[:CUT]
            sent_b[y, rel] = give[CUT:]
        return unused

    lax.fori_loop(0, 8, step, 0)


def own_kernel(me, tok, a0, a1, sent, b0, b1, acc):
    project(me, tok, functools.partial(block_of, (a0, a1, sent.at[0], sent.at[1], b0, b1)), acc)


def mean_kernel(me, tok, bend, own, a0, a1, a2, a3, b0, b1, sums, acc):
    project(me, tok, functools.partial(block_of, (a0, a1, a2, a3, b0, b1)), acc)
    c = jnp.zeros((448, 128), F32)
    s = jnp.zeros((448, 128), F32)
    for k in range(4):
        lanes = slice(128 * k, 128 * k + 128)
        mean = acc[:, lanes] / 32.0
        b = bend[:, lanes]
        off = own[:, lanes] - mean
        c += b * mean * mean
        s += b * off * off
    sums[0:1, :] = jnp.sum(c.T, axis=0, keepdims=True)
    sums[1:2, :] = jnp.sum(s.T, axis=0, keepdims=True)


def swap(value, axis):
    return lax.ppermute(value, axis, ((0, 1), (1, 0)))


def to_all(value, axis):
    count = lax.axis_size(axis)
    return lax.all_to_all(
        jnp.broadcast_to(value[None], (count, *value.shape)), axis, 0, 0, tiled=True
    )


def total(*values):
    return functools.reduce(jnp.add, [v.astype(F32) for v in values])


def shape(*lengths, dtype=BF):
    return jax.ShapeDtypeStruct(lengths, dtype)


def along_x(value, by):
    return lax.ppermute(value, "x", [(i, (i + by) % 4) for i in range(4)])


def shards(tokens, gate_weight, up_act, cotangent):
    me = jnp.stack([lax.axis_index("zl"), lax.axis_index("c"), lax.axis_index("x")])
    me = me.astype(jnp.int32)
    flops = 2 * 448 * 512 * 4096
    rest = 448 - CUT
    w0 = lax.all_gather(gate_weight.T, "y", axis=0)
    t0, w0 = lax.optimization_barrier((to_all(tokens, "zh"), w0))
    t3, t1 = along_x(t0, 1), along_x(t0, -1)
    w1 = swap(w0, "zl")
    t2a, t2b = along_x(t3[:2], 1), along_x(t1[2:], -1)
    w2, w3 = swap(w0, "c"), swap(w1, "c")
    tok, coeff, bend = call(
        gate_kernel,
        [shape(16, 512, 256), shape(448, 512), shape(448, 512, dtype=F32)],
        (me, t0, t1, t3, t2a, t2b, up_act.T, cotangent.T, w0, w1, w2, w3),
        flops,
        [pltpu.VMEM((448, 512), F32)],
    )
    a0, a1, sent, b0, sent_b = call(
        grad_kernel,
        [shape(8, CUT, 128)] * 2
        + [shape(2, 8, CUT, 128)]
        + [shape(8, 2, rest, 128)] * 2,
        (me, tok, coeff),
        flops,
    )
    across_b = lax.all_to_all(total(b0, swap(sent_b, "c")).astype(BF), "y", 0, 0, tiled=True)
    came = swap(sent, "c")
    came_1 = swap(total(a1, came[1]).astype(BF), "zl")
    sums_a = total(a0, came[0], came_1).astype(BF)
    own = call(
        own_kernel, [shape(448, 512, dtype=F32)], (me, tok, a0, a1, sent, b0, sent_b), flops
    )[0]
    sums_a, across_b, own = lax.optimization_barrier((sums_a, across_b, own))
    across_a = lax.all_to_all(sums_a, "y", 0, 0, tiled=True)
    part_b = jnp.sum(across_b.astype(F32), axis=0).astype(BF)
    other_b = swap(part_b, "zl")
    both_b = total(part_b, other_b[::-1]).astype(BF)
    grad_a = jnp.sum(across_a.astype(F32), axis=0).astype(BF)
    u0, both_b = lax.optimization_barrier((to_all(grad_a, "y"), both_b))
    v0 = to_all(both_b, "y")
    u1 = swap(u0, "zl")
    u2, u3 = swap(u0, "c"), swap(u1, "c")
    v1 = swap(v0, "c")
    line = call(
        mean_kernel,
        [shape(2, 448, dtype=F32)],
        (me, tok, bend, own, u0, u1, u2, u3, v0, v1),
        flops,
        [pltpu.VMEM((448, 512), F32)],
    )[0]
    whole = jnp.sum(to_all(line, REP), axis=0)
    grad = jnp.concatenate([grad_a, both_b[0]], axis=0).T
    return grad, whole[0], whole[1] / 31


def solution(mesh):
    torus = Mesh(mesh.devices.reshape(8, 2, 2, 4, 4), ("y", "zl", "c", "zh", "x"))
    fsdp = ("zh", "x")
    return jax.shard_map(
        shards,
        mesh=torus,
        in_specs=(P(REP, fsdp),) * 4,
        out_specs=(P(REP, fsdp), P(fsdp), P(fsdp)),
        check_vma=False,
    )
```

```python
import functools

import jax
import jax.numpy as jnp
from jax import lax
from jax.experimental import pallas as pl
from jax.experimental.pallas import tpu as pltpu
from jax.sharding import Mesh
from jax.sharding import PartitionSpec as P

REP = ("y", "zl", "c")
F32, BF = jnp.float32, jnp.bfloat16
NT = (((1,), (1,)), ((), ()))
CUT = 336
VMEM_LIMIT = 60 * 1024 * 1024
TOK = pltpu.VMEM((16, 512, 256), BF)
ACC = pltpu.VMEM((448, 512), F32)
VM = pl.BlockSpec(memory_space=pltpu.VMEM)
ANY = pl.BlockSpec(memory_space=pltpu.HBM)
SM = pl.BlockSpec(memory_space=pltpu.SMEM)


def call(kernel, outs, operands, flops, scratch, anywhere=(), out_anywhere=()):
    moved = sum(a.size * a.dtype.itemsize for a in operands) + sum(
        o.size * o.dtype.itemsize for o in outs
    )
    ins = [SM] + [ANY if i in anywhere else VM for i in range(1, len(operands))]
    return pl.pallas_call(
        kernel,
        out_shape=outs,
        in_specs=ins,
        out_specs=[ANY if i in out_anywhere else VM for i in range(len(outs))],
        scratch_shapes=list(scratch),
        cost_estimate=pl.CostEstimate(flops=flops, bytes_accessed=moved, transcendentals=0),
        compiler_params=pltpu.CompilerParams(vmem_limit_bytes=VMEM_LIMIT),
    )(*operands)


def block_of(refs, y, rel):
    a0, a1, a2, a3, b0, b1 = refs
    own, other = ((a0, a2), (a1, a3))[rel]
    return (
        jnp.concatenate([own[y], b0[y, rel]], 0),
        jnp.concatenate([other[y], b1[y, rel]], 0),
    )


def project(me, tok, block, acc, ready=None):
    mine, first = me[0], me[1] == 0
    acc[...] = jnp.zeros_like(acc)

    def step(y, unused):
        if ready is not None:
            ready(y)
        rows, cols = [], []
        for rel in (0, 1):
            own, other = block(y, rel)
            rows += [jnp.where(first, own, other), jnp.where(first, other, own)]
            cols.append(tok[2 * y + jnp.bitwise_xor(mine, rel)])
        acc[...] += lax.dot_general(
            jnp.concatenate(rows, 1), jnp.concatenate(cols, 1), NT, preferred_element_type=F32
        )
        return unused

    lax.fori_loop(0, 8, step, 0)


def fetch(source, tok, sems):
    def part(y):
        at = pl.ds(2 * y, 2)
        return pltpu.make_async_copy(source.at[at], tok.at[at], sems.at[y])

    for y in range(8):
        part(y).start()
    return lambda y: part(y).wait()


def first_kernel(*refs):
    me, t, zp, zm, z2a, z2b, x3, x1, o3, o1, fa, fb, up, cot, a0, a1, a2, a3, b0, b1 = refs[:20]
    tok_out, bend_out, own0, own1, sent, own_b, sent_b = refs[20:27]
    tok, coeff, bend, acc, sems, out_sems = refs[27:]
    mine, first = me[0], me[1] == 0
    copies = []

    def put(dx, dz, half, value):
        f = 4 * lax.rem(me[3] + dz, 4) + lax.rem(me[2] + dx, 4)
        there = tok.at[f, pl.ds(256 * half, 256), :]
        copies.append(pltpu.make_async_copy(value, there, sems.at[len(copies)]))

    for half in (0, 1):
        own = pl.ds(256 * half, 256)
        put(0, 0, half, t.at[own])
        put(0, 3, half, zp.at[own])
        put(0, 1, half, zm.at[own])
        put(0, 2, half, (z2a, z2b)[half])
        for dx, near, far in ((3, x3, o3), (1, x1, o1)):
            for i, dz in enumerate((0, 3, 1)):
                put(dx, dz, half, near.at[pl.ds(768 * half + 256 * i, 256)])
            put(dx, 2, half, far.at[own])
        for i, dz in enumerate((0, 3, 1, 2)):
            put(2, dz, half, (fa, fb)[half].at[pl.ds(256 * i, 256)])
    for copy in copies:
        copy.start()
    for copy in copies:
        copy.wait()
    keep_tok = pltpu.make_async_copy(tok, tok_out, out_sems.at[0])
    keep_tok.start()
    project(me, tok, functools.partial(block_of, (a0, a1, a2, a3, b0, b1)), acc)

    def part(i, unused):
        at = pl.ds(pl.multiple_of(i * 32, 32), 32)
        pre = acc[at, :]
        s = jax.nn.sigmoid(pre)
        one = s * (1.0 + pre * (1.0 - s))
        two = s * (1.0 - s) * (2.0 + pre * (1.0 - 2.0 * s))
        weighted = cot[at, :].astype(F32) * up[at, :].astype(F32)
        coeff[at, :] = (weighted * one).astype(BF)
        bend[at, :] = weighted * two
        return unused

    lax.fori_loop(0, 448 // 32, part, 0)
    keep_bend = pltpu.make_async_copy(bend, bend_out, out_sems.at[1])
    keep_bend.start()

    def step(y, unused):
        for rel, own in ((0, own0), (1, own1)):
            tile = tok[2 * y + jnp.bitwise_xor(mine, rel)]
            got = jnp.dot(coeff[...], tile, preferred_element_type=F32).astype(BF)
            low, high = got[:, :128], got[:, 128:]
            keep, give = jnp.where(first, low, high), jnp.where(first, high, low)
            own[y] = keep[:CUT]
            own_b[y, rel] = keep[CUT:]
            sent[rel, y] = give[:CUT]
            sent_b[y, rel] = give[CUT:]
        return unused

    lax.fori_loop(0, 8, step, 0)
    keep_tok.wait()
    keep_bend.wait()


def own_kernel(me, source, a0, a1, sent, b0, b1, acc, tok, sems):
    blocks = (a0, a1, sent.at[0], sent.at[1], b0, b1)
    project(me, tok, functools.partial(block_of, blocks), acc, fetch(source, tok, sems))


def mean_kernel(me, source, bend_in, own_in, a0, a1, a2, a3, b0, b1, sums, acc, bend, own, tok, sems):
    ready = fetch(source, tok, sems)
    get_bend = pltpu.make_async_copy(bend_in, bend, sems.at[8])
    get_own = pltpu.make_async_copy(own_in, own, sems.at[9])
    get_bend.start()
    get_own.start()
    project(me, tok, functools.partial(block_of, (a0, a1, a2, a3, b0, b1)), acc, ready)
    get_bend.wait()
    get_own.wait()
    c = jnp.zeros((448, 128), F32)
    s = jnp.zeros((448, 128), F32)
    for k in range(4):
        lanes = slice(128 * k, 128 * k + 128)
        mean = acc[:, lanes] / 32.0
        b = bend[:, lanes]
        off = own[:, lanes] - mean
        c += b * mean * mean
        s += b * off * off
    sums[0:1, :] = jnp.sum(c.T, axis=0, keepdims=True)
    sums[1:2, :] = jnp.sum(s.T, axis=0, keepdims=True)


def swap(value, axis):
    return lax.ppermute(value, axis, ((0, 1), (1, 0)))


def to_all(value, axis):
    count = lax.axis_size(axis)
    return lax.all_to_all(
        jnp.broadcast_to(value[None], (count, *value.shape)), axis, 0, 0, tiled=True
    )


def total(*values):
    return functools.reduce(jnp.add, [v.astype(F32) for v in values])


def shape(*lengths, dtype=BF):
    return jax.ShapeDtypeStruct(lengths, dtype)


def turn(value, axis, by):
    return lax.ppermute(value, axis, [(i, (i + by) % 4) for i in range(4)])


def all_features(t, weight_a, weight_b):
    zp, zm = turn(t, "zh", 1), turn(t, "zh", -1)
    three = (t, zp, zm)
    near = jnp.concatenate([v[:256] for v in three] + [v[256:] for v in three])
    x3, x1 = turn(near, "x", 1), turn(near, "x", -1)
    z2a, z2b = turn(zp[:256], "zh", 1), turn(zm[256:], "zh", -1)
    weights, (z2a, z2b) = all_rows(weight_a, weight_b, z2a, z2b)
    far = jnp.concatenate([z2a, z2b])
    o3, o1 = turn(far, "x", 1), turn(far, "x", -1)
    fa = turn(jnp.concatenate([x3[:768], o3[:256]]), "x", 1)
    fb = turn(jnp.concatenate([x1[768:], o1[256:]]), "x", -1)
    return (t, zp, zm, z2a, z2b, x3, x1, o3, o1, fa, fb), weights


def all_rows(part_a, part_b, *after):
    a0, part_b, *after = lax.optimization_barrier((to_all(part_a, "y"), part_b, *after))
    b0 = to_all(part_b, "y")
    a1 = swap(a0, "zl")
    return (a0, a1, swap(a0, "c"), swap(a1, "c"), b0, swap(b0, "c")), after


def shards(tokens, gate_weight, up_act, cotangent):
    me = jnp.stack([lax.axis_index(axis) for axis in ("zl", "c", "x", "zh")]).astype(jnp.int32)
    flops = 2 * 448 * 512 * 4096
    rest = 448 - CUT
    weight = gate_weight.T
    weight_b = jnp.stack([weight[CUT:], swap(weight[CUT:], "zl")])
    pieces, weights = all_features(tokens, weight[:CUT], weight_b)
    tok, bend, a0, a1, sent, b0, sent_b = call(
        first_kernel,
        [
            shape(16, 512, 256),
            shape(448, 512, dtype=F32),
            *[shape(8, CUT, 128)] * 2,
            shape(2, 8, CUT, 128),
            *[shape(8, 2, rest, 128)] * 2,
        ],
        (me, *pieces, up_act.T, cotangent.T, *weights),
        2 * flops,
        [TOK, pltpu.VMEM((448, 512), BF), *[ACC] * 2, *map(pltpu.SemaphoreType.DMA, ((32,), (2,)))],
        range(1, 12),
        (0, 1),
    )
    came_b = swap(sent_b, "c")
    sent, came_b = lax.optimization_barrier((sent, came_b))
    came = swap(sent, "c")
    across_b = lax.all_to_all(total(b0, came_b).astype(BF), "y", 0, 0, tiled=True)
    came_1 = swap(total(a1, came[1]).astype(BF), "zl")
    sums_a = total(a0, came[0], came_1).astype(BF)
    own = call(
        own_kernel,
        [shape(448, 512, dtype=F32)],
        (me, tok, a0, a1, sent, b0, sent_b),
        flops,
        [TOK, pltpu.SemaphoreType.DMA((8,))],
        (1,),
    )[0]
    sums_a, across_b, own = lax.optimization_barrier((sums_a, across_b, own))
    across_a = lax.all_to_all(sums_a, "y", 0, 0, tiled=True)
    part_b = jnp.sum(across_b.astype(F32), axis=0).astype(BF)
    other_b = swap(part_b, "zl")
    both_b = total(part_b, other_b[::-1]).astype(BF)
    grad_a = jnp.sum(across_a.astype(F32), axis=0).astype(BF)
    rows, _ = all_rows(grad_a, both_b)
    line = call(
        mean_kernel,
        [shape(2, 448, dtype=F32)],
        (me, tok, bend, own, *rows),
        flops,
        [*[ACC] * 3, TOK, pltpu.SemaphoreType.DMA((10,))],
        (1, 2, 3),
    )[0]
    whole = jnp.sum(to_all(line, REP), axis=0)
    grad = jnp.concatenate([grad_a, both_b[0]], axis=0).T
    return grad, whole[0], whole[1] / 31


def solution(mesh):
    torus = Mesh(mesh.devices.reshape(8, 2, 2, 4, 4), ("y", "zl", "c", "zh", "x"))
    fsdp = ("zh", "x")
    return jax.shard_map(
        shards,
        mesh=torus,
        in_specs=(P(REP, fsdp),) * 4,
        out_specs=(P(REP, fsdp), P(fsdp), P(fsdp)),
        check_vma=False,
    )
```

```python
import functools

import jax
import jax.numpy as jnp
from jax import lax
from jax.experimental import pallas as pl
from jax.experimental.pallas import tpu as pltpu
from jax.sharding import Mesh
from jax.sharding import PartitionSpec as P

REP = ("y", "zl", "c")
F32, BF = jnp.float32, jnp.bfloat16
NT = (((1,), (1,)), ((), ()))
CUT = 336
VMEM_LIMIT = 60 * 1024 * 1024
TOK = pltpu.VMEM((16, 512, 256), BF)
ACC = pltpu.VMEM((448, 512), F32)
VM = pl.BlockSpec(memory_space=pltpu.VMEM)
ANY = pl.BlockSpec(memory_space=pltpu.HBM)
SM = pl.BlockSpec(memory_space=pltpu.SMEM)


def call(kernel, outs, operands, flops, scratch, near=False):
    moved = sum(a.size * a.dtype.itemsize for a in operands) + sum(
        o.size * o.dtype.itemsize for o in outs
    )
    return pl.pallas_call(
        kernel,
        out_shape=outs,
        in_specs=[SM] + [ANY] * (len(operands) - 1),
        out_specs=[VM if near else ANY] * len(outs),
        scratch_shapes=list(scratch),
        cost_estimate=pl.CostEstimate(flops=flops, bytes_accessed=moved, transcendentals=0),
        compiler_params=pltpu.CompilerParams(vmem_limit_bytes=VMEM_LIMIT),
    )(*operands)


def fetched(pairs, sems):
    def part(i, y):
        source, there = pairs[i]
        return pltpu.make_async_copy(source.at[y], there.at[y], sems.at[i, y])

    for y in range(8):
        for i in range(len(pairs)):
            part(i, y).start()

    def ready(y):
        for i in range(len(pairs)):
            part(i, y).wait()

    return ready


def rows_of(held, held_b, y, rel):
    own, other = held[rel, y], held[2 + rel, y]
    if held_b is None:
        return own, other
    return (
        jnp.concatenate([own, held_b[0, y, rel]], 0),
        jnp.concatenate([other, held_b[1, y, rel]], 0),
    )


def project(me, tok, held, held_b, acc, ready):
    mine, first = me[0], me[1] == 0

    def product(y):
        ready(y)
        rows, cols = [], []
        for rel in (0, 1):
            own, other = rows_of(held, held_b, y, rel)
            rows += [jnp.where(first, own, other), jnp.where(first, other, own)]
            cols.append(tok[2 * y + jnp.bitwise_xor(mine, rel)])
        return lax.dot_general(
            jnp.concatenate(rows, 1), jnp.concatenate(cols, 1), NT, preferred_element_type=F32
        )

    acc[...] = product(0)

    def step(y, unused):
        acc[...] += product(y)
        return unused

    lax.fori_loop(1, 8, step, 0)


def first_kernel(*refs):
    me, t0, p1, p2, m1, m2, f1, f2, up_in, cot_in, w0, w1, w2, w3 = refs[:14]
    tok_out, bend_out, *outs = refs[14:21]
    tok, held, up, cot, coeff, bend, acc, own, own_b, tok_sems, w_sems, in_sems, out_sems, sems = refs[21:]
    mine, first = me[0], me[1] == 0
    sources = ((t0.at[0:2], t0.at[2:4]), (m2, m1), (f1, f2), (p1, p2))

    def token_copy(d, z):
        there = tok.at[4 * z + lax.rem(me[2] + d, 4)]
        return pltpu.make_async_copy(sources[d][z // 2].at[z % 2], there, tok_sems.at[d, z])

    for d in (0, 1, 3, 2):
        for z in range(4):
            token_copy(d, z).start()
    w_ready = fetched([(w, held.at[i]) for i, w in enumerate((w0, w1, w2, w3))], w_sems)
    get_up = pltpu.make_async_copy(up_in, up, in_sems.at[0])
    get_cot = pltpu.make_async_copy(cot_in, cot, in_sems.at[1])
    get_up.start()
    get_cot.start()
    for d in (0, 1, 3, 2):
        for z in range(4):
            token_copy(d, z).wait()
    keep_tok = pltpu.make_async_copy(tok, tok_out, sems.at[0])
    keep_tok.start()
    project(me, tok, held, None, acc, w_ready)
    get_up.wait()
    get_cot.wait()

    def part(i, unused):
        at = pl.ds(pl.multiple_of(i * 32, 32), 32)
        pre = acc[at, :]
        s = jax.nn.sigmoid(pre)
        one = s * (1.0 + pre * (1.0 - s))
        two = s * (1.0 - s) * (2.0 + pre * (1.0 - 2.0 * s))
        weighted = cot[at, :].astype(F32) * up[at, :].astype(F32)
        coeff[at, :] = (weighted * one).astype(BF)
        bend[at, :] = weighted * two
        return unused

    lax.fori_loop(0, 448 // 32, part, 0)
    keep_bend = pltpu.make_async_copy(bend, bend_out, sems.at[1])
    keep_bend.start()

    def out_copies(y):
        pairs = [(own.at[k, y], out) for k, out in enumerate((outs[0].at[y], outs[1].at[y]))]
        pairs += [(own.at[2 + k, y], outs[2].at[k, y]) for k in range(2)]
        pairs += [(own_b.at[k, y], outs[3 + k].at[y]) for k in range(2)]
        return [
            pltpu.make_async_copy(here, there, out_sems.at[k, y])
            for k, (here, there) in enumerate(pairs)
        ]

    def step(y, unused):
        for rel in (0, 1):
            tile = tok[2 * y + jnp.bitwise_xor(mine, rel)]
            got = jnp.dot(coeff[...], tile, preferred_element_type=F32).astype(BF)
            low, high = got[:, :128], got[:, 128:]
            keep, give = jnp.where(first, low, high), jnp.where(first, high, low)
            own[rel, y] = keep[:CUT]
            own_b[0, y, rel] = keep[CUT:]
            own[2 + rel, y] = give[:CUT]
            own_b[1, y, rel] = give[CUT:]
        for copy in out_copies(y):
            copy.start()
        return unused

    lax.fori_loop(0, 8, step, 0)
    for y in range(8):
        for copy in out_copies(y):
            copy.wait()
    keep_tok.wait()
    keep_bend.wait()


def fetch_all(source, arrays, tok, held, held_b, tok_sems, sems):
    pairs = [(a, held.at[i]) for i, a in enumerate(arrays[:4])]
    pairs += [(b, held_b.at[i]) for i, b in enumerate(arrays[4:])]

    def part(y):
        at = pl.ds(2 * y, 2)
        return pltpu.make_async_copy(source.at[at], tok.at[at], tok_sems.at[y])

    for y in range(8):
        part(y).start()
    rows_ready = fetched(pairs, sems)

    def ready(y):
        part(y).wait()
        rows_ready(y)

    return ready


def own_kernel(me, source, a0, a1, sent, b0, b1, acc, tok, held, held_b, tok_sems, sems):
    arrays = (a0, a1, sent.at[0], sent.at[1], b0, b1)
    ready = fetch_all(source, arrays, tok, held, held_b, tok_sems, sems)
    project(me, tok, held, held_b, acc, ready)


def mean_kernel(me, source, bend_in, own_in, *refs):
    sums, acc, bend, own, tok, held, held_b, tok_sems, sems, in_sems = refs[6:]
    ready = fetch_all(source, refs[:6], tok, held, held_b, tok_sems, sems)
    get_bend = pltpu.make_async_copy(bend_in, bend, in_sems.at[0])
    get_own = pltpu.make_async_copy(own_in, own, in_sems.at[1])
    get_bend.start()
    get_own.start()
    project(me, tok, held, held_b, acc, ready)
    get_bend.wait()
    get_own.wait()
    c = jnp.zeros((448, 128), F32)
    s = jnp.zeros((448, 128), F32)
    for k in range(4):
        lanes = slice(128 * k, 128 * k + 128)
        mean = acc[:, lanes] / 32.0
        b = bend[:, lanes]
        off = own[:, lanes] - mean
        c += b * mean * mean
        s += b * off * off
    sums[0:1, :] = jnp.sum(c.T, axis=0, keepdims=True)
    sums[1:2, :] = jnp.sum(s.T, axis=0, keepdims=True)


def swap(value, axis):
    return lax.ppermute(value, axis, ((0, 1), (1, 0)))


def to_all(value, axis):
    count = lax.axis_size(axis)
    return lax.all_to_all(
        jnp.broadcast_to(value[None], (count, *value.shape)), axis, 0, 0, tiled=True
    )


def total(*values):
    return functools.reduce(jnp.add, [v.astype(F32) for v in values])


def shape(*lengths, dtype=BF):
    return jax.ShapeDtypeStruct(lengths, dtype)


def along_x(value, by):
    return lax.ppermute(value, "x", [(i, (i + by) % 4) for i in range(4)])


def all_rows(part_a, part_b):
    a0, part_b = lax.optimization_barrier((to_all(part_a, "y"), part_b))
    b0 = to_all(part_b, "y")
    a1 = swap(a0, "zl")
    return a0, a1, swap(a0, "c"), swap(a1, "c"), b0, swap(b0, "c")


def shards(tokens, gate_weight, up_act, cotangent):
    me = jnp.stack([lax.axis_index(axis) for axis in ("zl", "c", "x")]).astype(jnp.int32)
    flops = 2 * 448 * 512 * 4096
    rest = 448 - CUT
    dma = pltpu.SemaphoreType.DMA
    held = [pltpu.VMEM((4, 8, CUT, 128), BF), pltpu.VMEM((2, 8, 2, rest, 128), BF)]
    w0 = lax.all_gather(gate_weight.T, "y", axis=0)
    t0, w0 = lax.optimization_barrier((to_all(tokens, "zh"), w0))
    low, high = t0[:2], t0[2:]
    p1, m1 = along_x(low, 1), along_x(high, -1)
    p2, m2 = along_x(high, 1), along_x(low, -1)
    f1, f2 = along_x(p1, 1), along_x(m1, -1)
    w1, f1, f2 = lax.optimization_barrier((swap(w0, "zl"), f1, f2))
    w0, p2, m2 = lax.optimization_barrier((w0, p2, m2))
    w2, w3 = swap(w0, "c"), swap(w1, "c")
    tok, bend, a0, a1, sent, b0, sent_b = call(
        first_kernel,
        [
            shape(16, 512, 256),
            shape(448, 512, dtype=F32),
            *[shape(8, CUT, 128)] * 2,
            shape(2, 8, CUT, 128),
            *[shape(8, 2, rest, 128)] * 2,
        ],
        (me, t0, p1, p2, m1, m2, f1, f2, up_act.T, cotangent.T, w0, w1, w2, w3),
        2 * flops,
        [
            TOK,
            pltpu.VMEM((4, 8, 448, 128), BF),
            *[pltpu.VMEM((448, 512), BF)] * 3,
            *[ACC] * 2,
            *held,
            *map(dma, ((4, 4), (4, 8), (2,), (6, 8), (2,))),
        ],
    )
    came_b = swap(sent_b, "c")
    came = swap(sent, "c")
    across_b = lax.all_to_all(total(b0, came_b).astype(BF), "y", 0, 0, tiled=True)
    came_1 = swap(total(a1, came[1]).astype(BF), "zl")
    sums_a = total(a0, came[0], came_1).astype(BF)
    own = call(
        own_kernel,
        [shape(448, 512, dtype=F32)],
        (me, tok, a0, a1, sent, b0, sent_b),
        flops,
        [TOK, *held, dma((8,)), dma((6, 8))],
        True,
    )[0]
    sums_a, across_b, own = lax.optimization_barrier((sums_a, across_b, own))
    across_a = lax.all_to_all(sums_a, "y", 0, 0, tiled=True)
    part_b = jnp.sum(across_b.astype(F32), axis=0).astype(BF)
    other_b = swap(part_b, "zl")
    both_b = total(part_b, other_b[::-1]).astype(BF)
    grad_a = jnp.sum(across_a.astype(F32), axis=0).astype(BF)
    line = call(
        mean_kernel,
        [shape(2, 448, dtype=F32)],
        (me, tok, bend, own, *all_rows(grad_a, both_b)),
        flops,
        [*[ACC] * 3, TOK, *held, dma((8,)), dma((6, 8)), dma((2,))],
        True,
    )[0]
    whole = jnp.sum(to_all(line, REP), axis=0)
    grad = jnp.concatenate([grad_a, both_b[0]], axis=0).T
    return grad, whole[0], whole[1] / 31


def solution(mesh):
    torus = Mesh(mesh.devices.reshape(8, 2, 2, 4, 4), ("y", "zl", "c", "zh", "x"))
    fsdp = ("zh", "x")
    return jax.shard_map(
        shards,
        mesh=torus,
        in_specs=(P(REP, fsdp),) * 4,
        out_specs=(P(REP, fsdp), P(fsdp), P(fsdp)),
        check_vma=False,
    )
```

```python
import functools

import jax
import jax.numpy as jnp
from jax import lax
from jax.experimental import pallas as pl
from jax.experimental.pallas import tpu as pltpu
from jax.sharding import Mesh
from jax.sharding import PartitionSpec as P

REP = ("y", "zl", "c")
F32, BF = jnp.float32, jnp.bfloat16
NT = (((1,), (1,)), ((), ()))
CUT = 336
RING = 240
VMEM_LIMIT = 60 * 1024 * 1024
TOK = pltpu.VMEM((16, 512, 256), BF)
ACC = pltpu.VMEM((448, 512), F32)
VM = pl.BlockSpec(memory_space=pltpu.VMEM)
ANY = pl.BlockSpec(memory_space=pltpu.HBM)
SM = pl.BlockSpec(memory_space=pltpu.SMEM)


def call(kernel, outs, operands, flops, scratch, near=False):
    moved = sum(a.size * a.dtype.itemsize for a in operands) + sum(
        o.size * o.dtype.itemsize for o in outs
    )
    return pl.pallas_call(
        kernel,
        out_shape=outs,
        in_specs=[SM] + [ANY] * (len(operands) - 1),
        out_specs=[VM if near else ANY] * len(outs),
        scratch_shapes=list(scratch),
        cost_estimate=pl.CostEstimate(flops=flops, bytes_accessed=moved, transcendentals=0),
        compiler_params=pltpu.CompilerParams(vmem_limit_bytes=VMEM_LIMIT),
    )(*operands)


def fetched(pairs, sems):
    def part(i, half):
        source, there = pairs[i]
        count = source.shape[0] // 2
        at = pl.ds(count * half, count)
        return pltpu.make_async_copy(source.at[at], there.at[at], sems.at[i, half])

    for half in (0, 1):
        for i in range(len(pairs)):
            part(i, half).start()

    def ready(half):
        for i in range(len(pairs)):
            part(i, half).wait()

    return ready


def project(me, tok, rows_of, acc, ready):
    mine, first = me[0], me[1] == 0
    for half in (0, 1):
        ready(half)
        rows, cols = [], []
        for y in range(4 * half, 4 * half + 4):
            for rel in (0, 1):
                own, other = rows_of(y, rel)
                rows += [jnp.where(first, own, other), jnp.where(first, other, own)]
                cols.append(tok[2 * y + jnp.bitwise_xor(mine, rel)])
        part = lax.dot_general(
            jnp.concatenate(rows, 1), jnp.concatenate(cols, 1), NT, preferred_element_type=F32
        )
        acc[...] = part if half == 0 else acc[...] + part


def first_kernel(*refs):
    me, t0, p1, p2, m1, m2, f1, f2, up_in, cot_in, w0, w1, w2, w3 = refs[:14]
    tok_out, bend_out, *outs = refs[14:21]
    tok, held, up, cot, coeff, bend, acc, own, own_b, tok_sems, w_sems, in_sems, out_sems, sems = refs[21:]
    mine, first = me[0], me[1] == 0
    sources = ((t0.at[0:2], t0.at[2:4]), (m2, m1), (f1, f2), (p1, p2))

    def token_copy(d, z):
        there = tok.at[4 * z + lax.rem(me[2] + d, 4)]
        return pltpu.make_async_copy(sources[d][z // 2].at[z % 2], there, tok_sems.at[d, z])

    for z in range(4):
        for d in range(4):
            token_copy(d, z).start()
    w_ready = fetched([(w, held.at[i]) for i, w in enumerate((w0, w1, w2, w3))], w_sems)
    get_up = pltpu.make_async_copy(up_in, up, in_sems.at[0])
    get_cot = pltpu.make_async_copy(cot_in, cot, in_sems.at[1])
    get_up.start()
    get_cot.start()

    def ready(half):
        for z in (2 * half, 2 * half + 1):
            for d in range(4):
                token_copy(d, z).wait()
        w_ready(half)

    project(
        me, tok, lambda y, rel: (held[rel, y], held[2 + rel, y]), acc, ready
    )
    keep_tok = pltpu.make_async_copy(tok, tok_out, sems.at[0])
    keep_tok.start()
    get_up.wait()
    get_cot.wait()

    def part(i, unused):
        at = pl.ds(pl.multiple_of(i * 32, 32), 32)
        pre = acc[at, :]
        s = jax.nn.sigmoid(pre)
        one = s * (1.0 + pre * (1.0 - s))
        two = s * (1.0 - s) * (2.0 + pre * (1.0 - 2.0 * s))
        weighted = cot[at, :].astype(F32) * up[at, :].astype(F32)
        coeff[at, :] = (weighted * one).astype(BF)
        bend[at, :] = weighted * two
        return unused

    lax.fori_loop(0, 448 // 32, part, 0)
    keep_bend = pltpu.make_async_copy(bend, bend_out, sems.at[1])
    keep_bend.start()

    def out_copies(i):
        at = pl.ds(2 * i, 2)
        pairs = [(own.at[k, at], outs[k].at[at]) for k in range(2)]
        pairs += [(own.at[2 + k, at], outs[2].at[k, at]) for k in range(2)]
        pairs += [(own_b.at[k, at], outs[3 + k].at[at]) for k in range(2)]
        return [
            pltpu.make_async_copy(here, there, out_sems.at[k, i])
            for k, (here, there) in enumerate(pairs)
        ]

    for i in range(4):
        order = [(y, rel) for y in (2 * i, 2 * i + 1) for rel in (0, 1)]
        tiles = [tok[2 * y + jnp.bitwise_xor(mine, rel)] for y, rel in order]
        got = jnp.dot(
            coeff[...], jnp.concatenate(tiles, 1), preferred_element_type=F32
        ).astype(BF)
        for k, (y, rel) in enumerate(order):
            low, high = got[:, 256 * k : 256 * k + 128], got[:, 256 * k + 128 : 256 * k + 256]
            keep, give = jnp.where(first, low, high), jnp.where(first, high, low)
            own[rel, y] = keep[:CUT]
            own_b[0, y, rel] = keep[CUT:]
            own[2 + rel, y] = give[:CUT]
            own_b[1, y, rel] = give[CUT:]
        for copy in out_copies(i):
            copy.start()
    for i in range(4):
        for copy in out_copies(i):
            copy.wait()
    keep_tok.wait()
    keep_bend.wait()


def own_kernel(me, source, a0, a1, sent, b0, b1, acc, tok, held, held_b, tok_sems, sems):
    tok_ready = fetched([(source, tok)], tok_sems)
    pairs = [(a, held.at[i]) for i, a in enumerate((a0, a1, sent.at[0], sent.at[1]))]
    pairs += [(b, held_b.at[i]) for i, b in enumerate((b0, b1))]
    rows_ready = fetched(pairs, sems)

    def ready(half):
        tok_ready(half)
        rows_ready(half)

    def rows_of(y, rel):
        return [
            jnp.concatenate([held[2 * core + rel, y], held_b[core, y, rel]], 0) for core in (0, 1)
        ]

    project(me, tok, rows_of, acc, ready)


def mean_kernel(me, source, bend_in, own_in, *refs):
    sums, acc, bend, own, tok, held, held_b, tok_sems, sems, in_sems = refs[4:]
    tok_ready = fetched([(source, tok)], tok_sems)
    get_bend = pltpu.make_async_copy(bend_in, bend, in_sems.at[0])
    get_own = pltpu.make_async_copy(own_in, own, in_sems.at[1])
    pairs = [(a, (held, held_b)[i % 2].at[i // 2]) for i, a in enumerate(refs[:4])]
    rows_ready = fetched(pairs, sems)
    get_bend.start()
    get_own.start()

    def ready(half):
        tok_ready(half)
        rows_ready(half)

    def rows_of(y, rel):
        return [
            jnp.concatenate([held[core, y, rel], held_b[core, y, rel]], 0) for core in (0, 1)
        ]

    project(me, tok, rows_of, acc, ready)
    get_bend.wait()
    get_own.wait()
    c = jnp.zeros((448, 128), F32)
    s = jnp.zeros((448, 128), F32)
    for k in range(4):
        lanes = slice(128 * k, 128 * k + 128)
        mean = acc[:, lanes] / 32.0
        b = bend[:, lanes]
        off = own[:, lanes] - mean
        c += b * mean * mean
        s += b * off * off
    sums[0:1, :] = jnp.sum(c.T, axis=0, keepdims=True)
    sums[1:2, :] = jnp.sum(s.T, axis=0, keepdims=True)


def swap(value, axis):
    return lax.ppermute(value, axis, ((0, 1), (1, 0)))


def to_all(value, axis):
    count = lax.axis_size(axis)
    return lax.all_to_all(
        jnp.broadcast_to(value[None], (count, *value.shape)), axis, 0, 0, tiled=True
    )


def total(*values):
    return functools.reduce(jnp.add, [v.astype(F32) for v in values])


def shape(*lengths, dtype=BF):
    return jax.ShapeDtypeStruct(lengths, dtype)


def along_x(value, by):
    return lax.ppermute(value, "x", [(i, (i + by) % 4) for i in range(4)])


def shards(tokens, gate_weight, up_act, cotangent):
    me = jnp.stack([lax.axis_index(axis) for axis in ("zl", "c", "x")]).astype(jnp.int32)
    flops = 2 * 448 * 512 * 4096
    rest = 448 - CUT
    dma = pltpu.SemaphoreType.DMA
    held = [pltpu.VMEM((4, 8, CUT, 128), BF), pltpu.VMEM((2, 8, 2, rest, 128), BF)]
    w0 = lax.all_gather(gate_weight.T, "y", axis=0)
    t0, w0 = lax.optimization_barrier((to_all(tokens, "zh"), w0))
    low, high = t0[:2], t0[2:]
    p1, m1 = along_x(low, 1), along_x(high, -1)
    p2, m2 = along_x(high, 1), along_x(low, -1)
    f1, f2 = along_x(p1, 1), along_x(m1, -1)
    w1, f1, f2 = lax.optimization_barrier((swap(w0, "zl"), f1, f2))
    w0, p2, m2 = lax.optimization_barrier((w0, p2, m2))
    w2, w3 = swap(w0, "c"), swap(w1, "c")
    tok, bend, a0, a1, sent, b0, sent_b = call(
        first_kernel,
        [
            shape(16, 512, 256),
            shape(448, 512, dtype=F32),
            *[shape(8, CUT, 128)] * 2,
            shape(2, 8, CUT, 128),
            *[shape(8, 2, rest, 128)] * 2,
        ],
        (me, t0, p1, p2, m1, m2, f1, f2, up_act.T, cotangent.T, w0, w1, w2, w3),
        2 * flops,
        [
            TOK,
            pltpu.VMEM((4, 8, 448, 128), BF),
            *[pltpu.VMEM((448, 512), BF)] * 3,
            *[ACC] * 2,
            *held,
            *map(dma, ((4, 4), (4, 2), (2,), (6, 4), (2,))),
        ],
    )
    came_b, came = swap(sent_b, "c"), swap(sent, "c")
    sums_b, came = lax.optimization_barrier((total(b0, came_b).astype(BF), came))
    across_b = lax.all_to_all(sums_b, "y", 0, 0, tiled=True)
    came_1 = swap(total(a1, came[1]).astype(BF), "zl")
    sums_a = total(a0, came[0], came_1).astype(BF)
    own = call(
        own_kernel,
        [shape(448, 512, dtype=F32)],
        (me, tok, a0, a1, sent, b0, sent_b),
        flops,
        [TOK, *held, dma((1, 2)), dma((6, 2))],
        True,
    )[0]
    sums_a, across_b, own = lax.optimization_barrier((sums_a, across_b, own))
    across_a = lax.all_to_all(sums_a, "y", 0, 0, tiled=True)
    part_b = jnp.sum(across_b.astype(F32), axis=0).astype(BF)
    other_b = swap(part_b, "zl")
    both_b = total(part_b, other_b[::-1]).astype(BF)
    grad_a = jnp.sum(across_a.astype(F32), axis=0).astype(BF)
    both_a = jnp.stack([grad_a, swap(grad_a, "zl")])
    both = jnp.concatenate([both_a, both_b], axis=1)
    g1 = to_all(both[:, RING:], "y")
    g0 = lax.all_gather(both[:, :RING], "y", axis=0)
    line = call(
        mean_kernel,
        [shape(2, 448, dtype=F32)],
        (me, tok, bend, own, g0, g1, swap(g0, "c"), swap(g1, "c")),
        flops,
        [
            *[ACC] * 3,
            TOK,
            pltpu.VMEM((2, 8, 2, RING, 128), BF),
            pltpu.VMEM((2, 8, 2, 448 - RING, 128), BF),
            *map(dma, ((1, 2), (4, 2), (2,))),
        ],
        True,
    )[0]
    whole = jnp.sum(to_all(line, REP), axis=0)
    grad = both[0].T
    return grad, whole[0], whole[1] / 31


def solution(mesh):
    torus = Mesh(mesh.devices.reshape(8, 2, 2, 4, 4), ("y", "zl", "c", "zh", "x"))
    fsdp = ("zh", "x")
    return jax.shard_map(
        shards,
        mesh=torus,
        in_specs=(P(REP, fsdp),) * 4,
        out_specs=(P(REP, fsdp), P(fsdp), P(fsdp)),
        check_vma=False,
    )
```

```python
import functools

import jax
import jax.numpy as jnp
from jax import lax
from jax.experimental import pallas as pl
from jax.experimental.pallas import tpu as pltpu
from jax.sharding import Mesh
from jax.sharding import PartitionSpec as P

REP = ("y", "zl", "c")
F32, BF = jnp.float32, jnp.bfloat16
NT = (((1,), (1,)), ((), ()))
CUT = 304
VMEM_LIMIT = 60 * 1024 * 1024
TOK = pltpu.VMEM((16, 512, 256), BF)
ACC = pltpu.VMEM((448, 512), F32)
VM = pl.BlockSpec(memory_space=pltpu.VMEM)
ANY = pl.BlockSpec(memory_space=pltpu.HBM)
SM = pl.BlockSpec(memory_space=pltpu.SMEM)


def call(kernel, outs, operands, flops, scratch, near=False):
    moved = sum(a.size * a.dtype.itemsize for a in operands) + sum(
        o.size * o.dtype.itemsize for o in outs
    )
    return pl.pallas_call(
        kernel,
        out_shape=outs,
        in_specs=[SM] + [ANY] * (len(operands) - 1),
        out_specs=[VM if near else ANY] * len(outs),
        scratch_shapes=list(scratch),
        cost_estimate=pl.CostEstimate(flops=flops, bytes_accessed=moved, transcendentals=0),
        compiler_params=pltpu.CompilerParams(vmem_limit_bytes=VMEM_LIMIT),
    )(*operands)


def fetched(pairs, sems):
    def part(i, half):
        source, there = pairs[i]
        count = source.shape[0] // 2
        at = pl.ds(count * half, count)
        return pltpu.make_async_copy(source.at[at], there.at[at], sems.at[i, half])

    for half in (0, 1):
        for i in range(len(pairs)):
            part(i, half).start()

    def ready(half):
        for i in range(len(pairs)):
            part(i, half).wait()

    return ready


def project(me, tok, rows_of, acc, ready):
    mine, first = me[0], me[1] == 0
    for half in (0, 1):
        ready(half)
        rows, cols = [], []
        for y in range(4 * half, 4 * half + 4):
            for rel in (0, 1):
                own, other = rows_of(y, rel)
                rows += [jnp.where(first, own, other), jnp.where(first, other, own)]
                cols.append(tok[2 * y + jnp.bitwise_xor(mine, rel)])
        part = lax.dot_general(
            jnp.concatenate(rows, 1), jnp.concatenate(cols, 1), NT, preferred_element_type=F32
        )
        acc[...] = part if half == 0 else acc[...] + part


def first_kernel(*refs):
    me, t0, p1, p2, m1, m2, f1, f2, up_in, cot_in, w0, w1, w2, w3 = refs[:14]
    tok_out, bend_out, *outs = refs[14:21]
    tok, held, up, cot, coeff, bend, acc, own, own_b, tok_sems, w_sems, in_sems, out_sems, sems = refs[21:]
    mine, first = me[0], me[1] == 0
    sources = ((t0.at[0:2], t0.at[2:4]), (m2, m1), (f1, f2), (p1, p2))

    def token_copy(d, z):
        there = tok.at[4 * z + lax.rem(me[2] + d, 4)]
        return pltpu.make_async_copy(sources[d][z // 2].at[z % 2], there, tok_sems.at[d, z])

    for z in range(4):
        for d in range(4):
            token_copy(d, z).start()
    w_ready = fetched([(w, held.at[i]) for i, w in enumerate((w0, w1, w2, w3))], w_sems)
    get_up = pltpu.make_async_copy(up_in, up, in_sems.at[0])
    get_cot = pltpu.make_async_copy(cot_in, cot, in_sems.at[1])
    get_up.start()
    get_cot.start()

    def ready(half):
        for z in (2 * half, 2 * half + 1):
            for d in range(4):
                token_copy(d, z).wait()
        w_ready(half)

    project(
        me, tok, lambda y, rel: (held[rel, y], held[2 + rel, y]), acc, ready
    )
    keep_tok = pltpu.make_async_copy(tok, tok_out, sems.at[0])
    keep_tok.start()
    get_up.wait()
    get_cot.wait()

    def part(i, unused):
        at = pl.ds(pl.multiple_of(i * 32, 32), 32)
        pre = acc[at, :]
        s = jax.nn.sigmoid(pre)
        one = s * (1.0 + pre * (1.0 - s))
        two = s * (1.0 - s) * (2.0 + pre * (1.0 - 2.0 * s))
        weighted = cot[at, :].astype(F32) * up[at, :].astype(F32)
        coeff[at, :] = (weighted * one).astype(BF)
        bend[at, :] = weighted * two
        return unused

    lax.fori_loop(0, 448 // 32, part, 0)
    keep_bend = pltpu.make_async_copy(bend, bend_out, sems.at[1])
    keep_bend.start()

    def out_copies(i):
        at = pl.ds(2 * i, 2)
        pairs = [(own.at[k, at], outs[k].at[at]) for k in range(2)]
        pairs += [(own.at[2 + k, at], outs[2].at[k, at]) for k in range(2)]
        pairs += [(own_b.at[k, at], outs[3 + k].at[at]) for k in range(2)]
        return [
            pltpu.make_async_copy(here, there, out_sems.at[k, i])
            for k, (here, there) in enumerate(pairs)
        ]

    for i in range(4):
        order = [(y, rel) for y in (2 * i, 2 * i + 1) for rel in (0, 1)]
        tiles = [tok[2 * y + jnp.bitwise_xor(mine, rel)] for y, rel in order]
        got = jnp.dot(
            coeff[...], jnp.concatenate(tiles, 1), preferred_element_type=F32
        ).astype(BF)
        for k, (y, rel) in enumerate(order):
            low, high = got[:, 256 * k : 256 * k + 128], got[:, 256 * k + 128 : 256 * k + 256]
            keep, give = jnp.where(first, low, high), jnp.where(first, high, low)
            own[rel, y] = keep[:CUT]
            own_b[0, y, rel] = keep[CUT:]
            own[2 + rel, y] = give[:CUT]
            own_b[1, y, rel] = give[CUT:]
        for copy in out_copies(i):
            copy.start()
    for i in range(4):
        for copy in out_copies(i):
            copy.wait()
    keep_tok.wait()
    keep_bend.wait()


def both_parts(held, held_b, y, rel):
    return [jnp.concatenate([held[2 * core + rel, y], held_b[core, y, rel]], 0) for core in (0, 1)]


def own_kernel(me, source, a0, a1, sent, b0, b1, acc, tok, held, held_b, tok_sems, sems):
    tok_ready = fetched([(source, tok)], tok_sems)
    pairs = [(a, held.at[i]) for i, a in enumerate((a0, a1, sent.at[0], sent.at[1]))]
    pairs += [(b, held_b.at[i]) for i, b in enumerate((b0, b1))]
    rows_ready = fetched(pairs, sems)

    def ready(half):
        tok_ready(half)
        rows_ready(half)

    project(me, tok, functools.partial(both_parts, held, held_b), acc, ready)


def mean_kernel(me, source, bend_in, own_in, *refs):
    sums, acc, bend, own, tok, held, held_b, tok_sems, sems, in_sems = refs[6:]
    tok_ready = fetched([(source, tok)], tok_sems)
    get_bend = pltpu.make_async_copy(bend_in, bend, in_sems.at[0])
    get_own = pltpu.make_async_copy(own_in, own, in_sems.at[1])
    pairs = [(a, held.at[i]) for i, a in enumerate(refs[:4])]
    pairs += [(b, held_b.at[i]) for i, b in enumerate(refs[4:6])]
    rows_ready = fetched(pairs, sems)
    get_bend.start()
    get_own.start()

    def ready(half):
        tok_ready(half)
        rows_ready(half)

    project(me, tok, functools.partial(both_parts, held, held_b), acc, ready)
    get_bend.wait()
    get_own.wait()
    c = jnp.zeros((448, 128), F32)
    s = jnp.zeros((448, 128), F32)
    for k in range(4):
        lanes = slice(128 * k, 128 * k + 128)
        mean = acc[:, lanes] / 32.0
        b = bend[:, lanes]
        off = own[:, lanes] - mean
        c += b * mean * mean
        s += b * off * off
    sums[0:1, :] = jnp.sum(c.T, axis=0, keepdims=True)
    sums[1:2, :] = jnp.sum(s.T, axis=0, keepdims=True)


def swap(value, axis):
    return lax.ppermute(value, axis, ((0, 1), (1, 0)))


def to_all(value, axis):
    count = lax.axis_size(axis)
    return lax.all_to_all(
        jnp.broadcast_to(value[None], (count, *value.shape)), axis, 0, 0, tiled=True
    )


def total(*values):
    return functools.reduce(jnp.add, [v.astype(F32) for v in values])


def shape(*lengths, dtype=BF):
    return jax.ShapeDtypeStruct(lengths, dtype)


def along_x(value, by):
    return lax.ppermute(value, "x", [(i, (i + by) % 4) for i in range(4)])


def shards(tokens, gate_weight, up_act, cotangent):
    me = jnp.stack([lax.axis_index(axis) for axis in ("zl", "c", "x")]).astype(jnp.int32)
    flops = 2 * 448 * 512 * 4096
    rest = 448 - CUT
    dma = pltpu.SemaphoreType.DMA
    held = [pltpu.VMEM((4, 8, CUT, 128), BF), pltpu.VMEM((2, 8, 2, rest, 128), BF)]
    w0 = lax.all_gather(gate_weight.T, "y", axis=0)
    t0, w0 = lax.optimization_barrier((to_all(tokens, "zh"), w0))
    low, high = t0[:2], t0[2:]
    p1, m1 = along_x(low, 1), along_x(high, -1)
    p2, m2 = along_x(high, 1), along_x(low, -1)
    f1, f2 = along_x(p1, 1), along_x(m1, -1)
    w1, f1, f2 = lax.optimization_barrier((swap(w0, "zl"), f1, f2))
    w0, p2, m2 = lax.optimization_barrier((w0, p2, m2))
    w2, w3 = swap(w0, "c"), swap(w1, "c")
    tok, bend, a0, a1, sent, b0, sent_b = call(
        first_kernel,
        [
            shape(16, 512, 256),
            shape(448, 512, dtype=F32),
            *[shape(8, CUT, 128)] * 2,
            shape(2, 8, CUT, 128),
            *[shape(8, 2, rest, 128)] * 2,
        ],
        (me, t0, p1, p2, m1, m2, f1, f2, up_act.T, cotangent.T, w0, w1, w2, w3),
        2 * flops,
        [
            TOK,
            pltpu.VMEM((4, 8, 448, 128), BF),
            *[pltpu.VMEM((448, 512), BF)] * 3,
            *[ACC] * 2,
            *held,
            *map(dma, ((4, 4), (4, 2), (2,), (6, 4), (2,))),
        ],
    )
    came_b, came = swap(sent_b, "c"), swap(sent, "c")
    sums_b, came = lax.optimization_barrier((total(b0, came_b).astype(BF), came))
    across_b = lax.all_to_all(sums_b, "y", 0, 0, tiled=True)
    came_1 = swap(total(a1, came[1]).astype(BF), "zl")
    sums_a = total(a0, came[0], came_1).astype(BF)
    own = call(
        own_kernel,
        [shape(448, 512, dtype=F32)],
        (me, tok, a0, a1, sent, b0, sent_b),
        flops,
        [TOK, *held, dma((1, 2)), dma((6, 2))],
        True,
    )[0]
    sums_a, across_b, own = lax.optimization_barrier((sums_a, across_b, own))
    across_a = lax.all_to_all(sums_a, "y", 0, 0, tiled=True)
    part_b = jnp.sum(across_b.astype(F32), axis=0).astype(BF)
    other_b = swap(part_b, "zl")
    both_b = total(part_b, other_b[::-1]).astype(BF)
    grad_a = jnp.sum(across_a.astype(F32), axis=0).astype(BF)
    u0, both_b = lax.optimization_barrier((to_all(grad_a, "y"), both_b))
    v0 = to_all(both_b, "y")
    u1 = swap(u0, "zl")
    rows = (u0, u1, swap(u0, "c"), swap(u1, "c"), v0, swap(v0, "c"))
    line = call(
        mean_kernel,
        [shape(2, 448, dtype=F32)],
        (me, tok, bend, own, *rows),
        flops,
        [*[ACC] * 3, TOK, *held, *map(dma, ((1, 2), (6, 2), (2,)))],
        True,
    )[0]
    whole = jnp.sum(to_all(line, REP), axis=0)
    grad = jnp.concatenate([grad_a, both_b[0]], axis=0).T
    return grad, whole[0], whole[1] / 31


def solution(mesh):
    torus = Mesh(mesh.devices.reshape(8, 2, 2, 4, 4), ("y", "zl", "c", "zh", "x"))
    fsdp = ("zh", "x")
    return jax.shard_map(
        shards,
        mesh=torus,
        in_specs=(P(REP, fsdp),) * 4,
        out_specs=(P(REP, fsdp), P(fsdp), P(fsdp)),
        check_vma=False,
    )
```

```python
import functools

import jax
import jax.numpy as jnp
from jax import lax
from jax.experimental import pallas as pl
from jax.experimental.pallas import tpu as pltpu
from jax.sharding import Mesh
from jax.sharding import PartitionSpec as P

REP = ("y", "zl", "c")
F32, BF = jnp.float32, jnp.bfloat16
NT = (((1,), (1,)), ((), ()))
CUT = 304
VMEM_LIMIT = 60 * 1024 * 1024
TOK = pltpu.VMEM((16, 512, 256), BF)
ACC = pltpu.VMEM((448, 512), F32)
VM = pl.BlockSpec(memory_space=pltpu.VMEM)
ANY = pl.BlockSpec(memory_space=pltpu.HBM)
SM = pl.BlockSpec(memory_space=pltpu.SMEM)


def call(kernel, outs, operands, flops, scratch, near=False):
    moved = sum(a.size * a.dtype.itemsize for a in operands) + sum(
        o.size * o.dtype.itemsize for o in outs
    )
    return pl.pallas_call(
        kernel,
        out_shape=outs,
        in_specs=[SM] + [ANY] * (len(operands) - 1),
        out_specs=[VM if near else ANY] * len(outs),
        scratch_shapes=list(scratch),
        cost_estimate=pl.CostEstimate(flops=flops, bytes_accessed=moved, transcendentals=0),
        compiler_params=pltpu.CompilerParams(vmem_limit_bytes=VMEM_LIMIT),
    )(*operands)


def fetched(pairs, sems):
    def part(i, half):
        source, there = pairs[i]
        count = source.shape[0] // 2
        at = pl.ds(count * half, count)
        return pltpu.make_async_copy(source.at[at], there.at[at], sems.at[i, half])

    for half in (0, 1):
        for i in range(len(pairs)):
            part(i, half).start()

    def ready(half):
        for i in range(len(pairs)):
            part(i, half).wait()

    return ready


def project(me, tok, rows_of, acc, ready):
    mine, first = me[0], me[1] == 0
    for half in (0, 1):
        ready(half)
        rows, cols = [], []
        for y in range(4 * half, 4 * half + 4):
            for rel in (0, 1):
                own, other = rows_of(y, rel)
                rows += [jnp.where(first, own, other), jnp.where(first, other, own)]
                cols.append(tok[2 * y + jnp.bitwise_xor(mine, rel)])
        part = lax.dot_general(
            jnp.concatenate(rows, 1), jnp.concatenate(cols, 1), NT, preferred_element_type=F32
        )
        acc[...] = part if half == 0 else acc[...] + part


def first_kernel(*refs):
    me, t0, p1, p2, m1, m2, f1, f2, up_in, cot_in, w0, w1, *other = refs[:16]
    tok_out, bend_out, *outs = refs[16:23]
    tok, held, up, cot, coeff, bend, acc, own, own_b, tok_sems, w_sems, in_sems, out_sems, sems = refs[23:]
    mine, first = me[0], me[1] == 0
    sources = ((t0.at[0:2], t0.at[2:4]), (m2, m1), (f1, f2), (p1, p2))

    def token_copy(d, z):
        there = tok.at[4 * z + lax.rem(me[2] + d, 4)]
        return pltpu.make_async_copy(sources[d][z // 2].at[z % 2], there, tok_sems.at[d, z])

    for z in range(4):
        for d in range(4):
            token_copy(d, z).start()
    def row_copies(half):
        at = pl.ds(4 * half, 4)
        own_rows = (w0.at[at], w1.at[at], other[half], other[2 + half])
        return [
            pltpu.make_async_copy(w, held.at[i, at], w_sems.at[i, half])
            for i, w in enumerate(own_rows)
        ]

    for half in (0, 1):
        for copy in row_copies(half):
            copy.start()
    get_up = pltpu.make_async_copy(up_in, up, in_sems.at[0])
    get_cot = pltpu.make_async_copy(cot_in, cot, in_sems.at[1])
    get_up.start()
    get_cot.start()

    def ready(half):
        for z in (2 * half, 2 * half + 1):
            for d in range(4):
                token_copy(d, z).wait()
        for copy in row_copies(half):
            copy.wait()

    project(
        me, tok, lambda y, rel: (held[rel, y], held[2 + rel, y]), acc, ready
    )
    keep_tok = pltpu.make_async_copy(tok, tok_out, sems.at[0])
    keep_tok.start()
    get_up.wait()
    get_cot.wait()

    def part(i, unused):
        at = pl.ds(pl.multiple_of(i * 32, 32), 32)
        pre = acc[at, :]
        s = jax.nn.sigmoid(pre)
        one = s * (1.0 + pre * (1.0 - s))
        two = s * (1.0 - s) * (2.0 + pre * (1.0 - 2.0 * s))
        weighted = cot[at, :].astype(F32) * up[at, :].astype(F32)
        coeff[at, :] = (weighted * one).astype(BF)
        bend[at, :] = weighted * two
        return unused

    lax.fori_loop(0, 448 // 32, part, 0)
    keep_bend = pltpu.make_async_copy(bend, bend_out, sems.at[1])
    keep_bend.start()

    def out_copies(i):
        at = pl.ds(2 * i, 2)
        pairs = [(own.at[k, at], outs[k].at[at]) for k in range(2)]
        pairs += [(own.at[2 + k, at], outs[2].at[k, at]) for k in range(2)]
        pairs += [(own_b.at[k, at], outs[3 + k].at[at]) for k in range(2)]
        return [
            pltpu.make_async_copy(here, there, out_sems.at[k, i])
            for k, (here, there) in enumerate(pairs)
        ]

    for i in range(4):
        order = [(y, rel) for y in (2 * i, 2 * i + 1) for rel in (0, 1)]
        tiles = [tok[2 * y + jnp.bitwise_xor(mine, rel)] for y, rel in order]
        got = jnp.dot(
            coeff[...], jnp.concatenate(tiles, 1), preferred_element_type=F32
        ).astype(BF)
        for k, (y, rel) in enumerate(order):
            low, high = got[:, 256 * k : 256 * k + 128], got[:, 256 * k + 128 : 256 * k + 256]
            keep, give = jnp.where(first, low, high), jnp.where(first, high, low)
            own[rel, y] = keep[:CUT]
            own_b[0, y, rel] = keep[CUT:]
            own[2 + rel, y] = give[:CUT]
            own_b[1, y, rel] = give[CUT:]
        for copy in out_copies(i):
            copy.start()
    for i in range(4):
        for copy in out_copies(i):
            copy.wait()
    keep_tok.wait()
    keep_bend.wait()


def both_parts(held, held_b, y, rel):
    return [jnp.concatenate([held[2 * core + rel, y], held_b[core, y, rel]], 0) for core in (0, 1)]


def own_kernel(me, source, a0, a1, sent, b0, b1, acc, tok, held, held_b, tok_sems, sems):
    tok_ready = fetched([(source, tok)], tok_sems)
    pairs = [(a, held.at[i]) for i, a in enumerate((a0, a1, sent.at[0], sent.at[1]))]
    pairs += [(b, held_b.at[i]) for i, b in enumerate((b0, b1))]
    rows_ready = fetched(pairs, sems)

    def ready(half):
        tok_ready(half)
        rows_ready(half)

    project(me, tok, functools.partial(both_parts, held, held_b), acc, ready)


def mean_kernel(me, source, bend_in, own_in, *refs):
    sums, acc, bend, own, tok, held, held_b, tok_sems, sems, in_sems = refs[6:]
    tok_ready = fetched([(source, tok)], tok_sems)
    get_bend = pltpu.make_async_copy(bend_in, bend, in_sems.at[0])
    get_own = pltpu.make_async_copy(own_in, own, in_sems.at[1])
    pairs = [(a, held.at[i]) for i, a in enumerate(refs[:4])]
    pairs += [(b, held_b.at[i]) for i, b in enumerate(refs[4:6])]
    rows_ready = fetched(pairs, sems)
    get_bend.start()
    get_own.start()

    def ready(half):
        tok_ready(half)
        rows_ready(half)

    project(me, tok, functools.partial(both_parts, held, held_b), acc, ready)
    get_bend.wait()
    get_own.wait()
    c = jnp.zeros((448, 128), F32)
    s = jnp.zeros((448, 128), F32)
    for k in range(4):
        lanes = slice(128 * k, 128 * k + 128)
        mean = acc[:, lanes] / 32.0
        b = bend[:, lanes]
        off = own[:, lanes] - mean
        c += b * mean * mean
        s += b * off * off
    for k, terms in enumerate((c, s)):
        line = jnp.sum(terms.T, axis=0, keepdims=True)
        line = jnp.concatenate([line, jnp.zeros((1, 64), F32)], 1)
        for i in range(4):
            row = line[:, 128 * i : 128 * i + 128]
            sums[:, 4 * k + i : 4 * k + i + 1, :] = jnp.broadcast_to(row[None], (32, 1, 128))


def swap(value, axis):
    return lax.ppermute(value, axis, ((0, 1), (1, 0)))


def to_all(value, axis):
    count = lax.axis_size(axis)
    return lax.all_to_all(
        jnp.broadcast_to(value[None], (count, *value.shape)), axis, 0, 0, tiled=True
    )


def total(*values):
    return functools.reduce(jnp.add, [v.astype(F32) for v in values])


def shape(*lengths, dtype=BF):
    return jax.ShapeDtypeStruct(lengths, dtype)


def along_x(value, by):
    return lax.ppermute(value, "x", [(i, (i + by) % 4) for i in range(4)])


def shards(tokens, gate_weight, up_act, cotangent):
    me = jnp.stack([lax.axis_index(axis) for axis in ("zl", "c", "x")]).astype(jnp.int32)
    flops = 2 * 448 * 512 * 4096
    rest = 448 - CUT
    dma = pltpu.SemaphoreType.DMA
    held = [pltpu.VMEM((4, 8, CUT, 128), BF), pltpu.VMEM((2, 8, 2, rest, 128), BF)]
    w0 = lax.all_gather(gate_weight.T, "y", axis=0)
    t0, w0 = lax.optimization_barrier((to_all(tokens, "zh"), w0))
    low, high = t0[:2], t0[2:]
    p1, m1 = along_x(low, 1), along_x(high, -1)
    p2, m2 = along_x(high, 1), along_x(low, -1)
    f1, f2 = along_x(p1, 1), along_x(m1, -1)
    w0, w1, p2, m2 = lax.optimization_barrier((w0, swap(w0, "zl"), p2, m2))
    other = [swap(w[at : at + 4], "c") for w in (w0, w1) for at in (0, 4)]
    tok, bend, a0, a1, sent, b0, sent_b = call(
        first_kernel,
        [
            shape(16, 512, 256),
            shape(448, 512, dtype=F32),
            *[shape(8, CUT, 128)] * 2,
            shape(2, 8, CUT, 128),
            *[shape(8, 2, rest, 128)] * 2,
        ],
        (me, t0, p1, p2, m1, m2, f1, f2, up_act.T, cotangent.T, w0, w1, *other),
        2 * flops,
        [
            TOK,
            pltpu.VMEM((4, 8, 448, 128), BF),
            *[pltpu.VMEM((448, 512), BF)] * 3,
            *[ACC] * 2,
            *held,
            *map(dma, ((4, 4), (4, 2), (2,), (6, 4), (2,))),
        ],
    )
    came_b, came = swap(sent_b, "c"), swap(sent, "c")
    sums_b, came = lax.optimization_barrier((total(b0, came_b).astype(BF), came))
    across_b = lax.all_to_all(sums_b, "y", 0, 0, tiled=True)
    came_1 = swap(total(a1, came[1]).astype(BF), "zl")
    sums_a = total(a0, came[0], came_1).astype(BF)
    own = call(
        own_kernel,
        [shape(448, 512, dtype=F32)],
        (me, tok, a0, a1, sent, b0, sent_b),
        flops,
        [TOK, *held, dma((1, 2)), dma((6, 2))],
        True,
    )[0]
    sums_a, across_b, own = lax.optimization_barrier((sums_a, across_b, own))
    across_a = lax.all_to_all(sums_a, "y", 0, 0, tiled=True)
    part_b = jnp.sum(across_b.astype(F32), axis=0).astype(BF)
    other_b = swap(part_b, "zl")
    both_b = total(part_b, other_b[::-1]).astype(BF)
    grad_a = jnp.sum(across_a.astype(F32), axis=0).astype(BF)
    u0, both_b = lax.optimization_barrier((to_all(grad_a, "y"), both_b))
    v0 = to_all(both_b, "y")
    u1 = swap(u0, "zl")
    rows = (u0, u1, swap(u0, "c"), swap(u1, "c"), v0, swap(v0, "c"))
    line = call(
        mean_kernel,
        [shape(32, 8, 128, dtype=F32)],
        (me, tok, bend, own, *rows),
        flops,
        [*[ACC] * 3, TOK, *held, *map(dma, ((1, 2), (6, 2), (2,)))],
        True,
    )[0]
    whole = jnp.sum(lax.all_to_all(line, REP, 0, 0, tiled=True), axis=0).reshape(2, 512)[:, :448]
    grad = jnp.concatenate([grad_a, both_b[0]], axis=0).T
    return grad, whole[0], whole[1] / 31


def solution(mesh):
    torus = Mesh(mesh.devices.reshape(8, 2, 2, 4, 4), ("y", "zl", "c", "zh", "x"))
    fsdp = ("zh", "x")
    return jax.shard_map(
        shards,
        mesh=torus,
        in_specs=(P(REP, fsdp),) * 4,
        out_specs=(P(REP, fsdp), P(fsdp), P(fsdp)),
        check_vma=False,
    )
```

```python
import functools

import jax
import jax.numpy as jnp
from jax import lax
from jax.experimental import pallas as pl
from jax.experimental.pallas import tpu as pltpu
from jax.sharding import Mesh
from jax.sharding import PartitionSpec as P

REP = ("y", "zl", "c")
F32, BF = jnp.float32, jnp.bfloat16
NT = (((1,), (1,)), ((), ()))
CUT = 256
BACK_CUT = 304
VMEM_LIMIT = 60 * 1024 * 1024
TOK = pltpu.VMEM((16, 512, 256), BF)
ACC = pltpu.VMEM((448, 512), F32)
VM = pl.BlockSpec(memory_space=pltpu.VMEM)
ANY = pl.BlockSpec(memory_space=pltpu.HBM)
SM = pl.BlockSpec(memory_space=pltpu.SMEM)


def call(kernel, outs, operands, flops, scratch, near=False):
    moved = sum(a.size * a.dtype.itemsize for a in operands) + sum(
        o.size * o.dtype.itemsize for o in outs
    )
    return pl.pallas_call(
        kernel,
        out_shape=outs,
        in_specs=[SM] + [ANY] * (len(operands) - 1),
        out_specs=[VM if near else ANY] * len(outs),
        scratch_shapes=list(scratch),
        cost_estimate=pl.CostEstimate(flops=flops, bytes_accessed=moved, transcendentals=0),
        compiler_params=pltpu.CompilerParams(vmem_limit_bytes=VMEM_LIMIT),
    )(*operands)


def fetched(pairs, sems):
    def part(i, half):
        source, there = pairs[i]
        count = source.shape[0] // 2
        at = pl.ds(count * half, count)
        return pltpu.make_async_copy(source.at[at], there.at[at], sems.at[i, half])

    for half in (0, 1):
        for i in range(len(pairs)):
            part(i, half).start()

    def ready(half):
        for i in range(len(pairs)):
            part(i, half).wait()

    return ready


def project(me, tok, rows_of, acc, ready):
    mine, first = me[0], me[1] == 0
    for half in (0, 1):
        ready(half)
        rows, cols = [], []
        for y in range(4 * half, 4 * half + 4):
            for rel in (0, 1):
                own, other = rows_of(y, rel)
                rows += [jnp.where(first, own, other), jnp.where(first, other, own)]
                cols.append(tok[2 * y + jnp.bitwise_xor(mine, rel)])
        part = lax.dot_general(
            jnp.concatenate(rows, 1), jnp.concatenate(cols, 1), NT, preferred_element_type=F32
        )
        acc[...] = part if half == 0 else acc[...] + part


def first_kernel(*refs):
    me, t0, p1, p2, m1, m2, f1, f2, up_in, cot_in, *weights = refs[:14]
    tok_out, bend_out, *outs = refs[14:21]
    tok, held, up, cot, coeff, bend, acc, own, own_b, tok_sems, w_sems, in_sems, out_sems, sems = refs[21:]
    mine, first = me[0], me[1] == 0
    sources = ((t0.at[0:2], t0.at[2:4]), (m2, m1), (f1, f2), (p1, p2))

    def token_copy(d, z):
        there = tok.at[4 * z + lax.rem(me[2] + d, 4)]
        return pltpu.make_async_copy(sources[d][z // 2].at[z % 2], there, tok_sems.at[d, z])

    for z in range(4):
        for d in range(4):
            token_copy(d, z).start()
    w_ready = fetched([(w, held.at[i]) for i, w in enumerate(weights)], w_sems)
    get_up = pltpu.make_async_copy(up_in, up, in_sems.at[0])
    get_cot = pltpu.make_async_copy(cot_in, cot, in_sems.at[1])
    get_up.start()
    get_cot.start()

    def ready(half):
        for z in (2 * half, 2 * half + 1):
            for d in range(4):
                token_copy(d, z).wait()
        w_ready(half)

    project(
        me, tok, lambda y, rel: (held[rel, y], held[2 + rel, y]), acc, ready
    )
    keep_tok = pltpu.make_async_copy(tok, tok_out, sems.at[0])
    keep_tok.start()
    get_up.wait()
    get_cot.wait()

    def part(i, unused):
        at = pl.ds(pl.multiple_of(i * 32, 32), 32)
        pre = acc[at, :]
        s = jax.nn.sigmoid(pre)
        one = s * (1.0 + pre * (1.0 - s))
        two = s * (1.0 - s) * (2.0 + pre * (1.0 - 2.0 * s))
        weighted = cot[at, :].astype(F32) * up[at, :].astype(F32)
        coeff[at, :] = (weighted * one).astype(BF)
        bend[at, :] = weighted * two
        return unused

    lax.fori_loop(0, 448 // 32, part, 0)
    keep_bend = pltpu.make_async_copy(bend, bend_out, sems.at[1])
    keep_bend.start()

    def out_copies(i):
        at = pl.ds(2 * i, 2)
        pairs = [(own.at[k, at], outs[k].at[at]) for k in range(2)]
        pairs += [(own.at[2 + k, at], outs[2].at[k, at]) for k in range(2)]
        pairs += [(own_b.at[k, at], outs[3 + k].at[at]) for k in range(2)]
        return [
            pltpu.make_async_copy(here, there, out_sems.at[k, i])
            for k, (here, there) in enumerate(pairs)
        ]

    for i in range(4):
        order = [(y, rel) for y in (2 * i, 2 * i + 1) for rel in (0, 1)]
        tiles = [tok[2 * y + jnp.bitwise_xor(mine, rel)] for y, rel in order]
        got = jnp.dot(
            coeff[...], jnp.concatenate(tiles, 1), preferred_element_type=F32
        ).astype(BF)
        for k, (y, rel) in enumerate(order):
            low, high = got[:, 256 * k : 256 * k + 128], got[:, 256 * k + 128 : 256 * k + 256]
            keep, give = jnp.where(first, low, high), jnp.where(first, high, low)
            own[rel, y] = keep[:CUT]
            own_b[0, y, rel] = keep[CUT:]
            own[2 + rel, y] = give[:CUT]
            own_b[1, y, rel] = give[CUT:]
        for copy in out_copies(i):
            copy.start()
    for i in range(4):
        for copy in out_copies(i):
            copy.wait()
    keep_tok.wait()
    keep_bend.wait()


def both_parts(held, held_b, y, rel):
    return [jnp.concatenate([held[2 * core + rel, y], held_b[core, y, rel]], 0) for core in (0, 1)]


def own_kernel(me, source, a0, a1, sent, b0, b1, acc, tok, held, held_b, tok_sems, sems):
    tok_ready = fetched([(source, tok)], tok_sems)
    pairs = [(a, held.at[i]) for i, a in enumerate((a0, a1, sent.at[0], sent.at[1]))]
    pairs += [(b, held_b.at[i]) for i, b in enumerate((b0, b1))]
    rows_ready = fetched(pairs, sems)

    def ready(half):
        tok_ready(half)
        rows_ready(half)

    project(me, tok, functools.partial(both_parts, held, held_b), acc, ready)


def mean_kernel(me, source, bend_in, own_in, *refs):
    sums, acc, bend, own, tok, held, held_b, tok_sems, sems, in_sems = refs[6:]
    tok_ready = fetched([(source, tok)], tok_sems)
    get_bend = pltpu.make_async_copy(bend_in, bend, in_sems.at[0])
    get_own = pltpu.make_async_copy(own_in, own, in_sems.at[1])
    pairs = [(a, held.at[i]) for i, a in enumerate(refs[:4])]
    pairs += [(b, held_b.at[i]) for i, b in enumerate(refs[4:6])]
    rows_ready = fetched(pairs, sems)
    get_bend.start()
    get_own.start()

    def ready(half):
        tok_ready(half)
        rows_ready(half)

    project(me, tok, functools.partial(both_parts, held, held_b), acc, ready)
    get_bend.wait()
    get_own.wait()
    c = jnp.zeros((448, 128), F32)
    s = jnp.zeros((448, 128), F32)
    for k in range(4):
        lanes = slice(128 * k, 128 * k + 128)
        mean = acc[:, lanes] / 32.0
        b = bend[:, lanes]
        off = own[:, lanes] - mean
        c += b * mean * mean
        s += b * off * off
    for k, terms in enumerate((c, s)):
        line = jnp.sum(terms.T, axis=0, keepdims=True)
        line = jnp.concatenate([line, jnp.zeros((1, 64), F32)], 1)
        for i in range(4):
            row = line[:, 128 * i : 128 * i + 128]
            sums[:, 4 * k + i : 4 * k + i + 1, :] = jnp.broadcast_to(row[None], (32, 1, 128))


def swap(value, axis):
    return lax.ppermute(value, axis, ((0, 1), (1, 0)))


def to_all(value, axis):
    count = lax.axis_size(axis)
    return lax.all_to_all(
        jnp.broadcast_to(value[None], (count, *value.shape)), axis, 0, 0, tiled=True
    )


def total(*values):
    return functools.reduce(jnp.add, [v.astype(F32) for v in values])


def shape(*lengths, dtype=BF):
    return jax.ShapeDtypeStruct(lengths, dtype)


def along_x(value, by):
    return lax.ppermute(value, "x", [(i, (i + by) % 4) for i in range(4)])


def shards(tokens, gate_weight, up_act, cotangent):
    me = jnp.stack([lax.axis_index(axis) for axis in ("zl", "c", "x")]).astype(jnp.int32)
    flops = 2 * 448 * 512 * 4096
    rest = 448 - CUT
    dma = pltpu.SemaphoreType.DMA
    held, held_back = (
        [pltpu.VMEM((4, 8, cut, 128), BF), pltpu.VMEM((2, 8, 2, 448 - cut, 128), BF)]
        for cut in (CUT, BACK_CUT)
    )
    w0 = lax.all_gather(gate_weight.T, "y", axis=0)
    t0, w0 = lax.optimization_barrier((to_all(tokens, "zh"), w0))
    low, high = t0[:2], t0[2:]
    p1, m1 = along_x(low, 1), along_x(high, -1)
    p2, m2 = along_x(high, 1), along_x(low, -1)
    f1, f2 = along_x(p1, 1), along_x(m1, -1)
    w1, f1, f2 = lax.optimization_barrier((swap(w0, "zl"), f1, f2))
    w0, p2, m2 = lax.optimization_barrier((w0, p2, m2))
    w2, w3 = swap(w0, "c"), swap(w1, "c")
    tok, bend, a0, a1, sent, b0, sent_b = call(
        first_kernel,
        [
            shape(16, 512, 256),
            shape(448, 512, dtype=F32),
            *[shape(8, CUT, 128)] * 2,
            shape(2, 8, CUT, 128),
            *[shape(8, 2, rest, 128)] * 2,
        ],
        (me, t0, p1, p2, m1, m2, f1, f2, up_act.T, cotangent.T, w0, w1, w2, w3),
        2 * flops,
        [
            TOK,
            pltpu.VMEM((4, 8, 448, 128), BF),
            *[pltpu.VMEM((448, 512), BF)] * 3,
            *[ACC] * 2,
            *held,
            *map(dma, ((4, 4), (4, 2), (2,), (6, 4), (2,))),
        ],
    )
    came_b, came = swap(sent_b, "c"), swap(sent, "c")
    sums_b, came = lax.optimization_barrier((total(b0, came_b).astype(BF), came))
    across_b = lax.all_to_all(sums_b, "y", 0, 0, tiled=True)
    came_1 = swap(total(a1, came[1]).astype(BF), "zl")
    sums_a = total(a0, came[0], came_1).astype(BF)
    own = call(
        own_kernel,
        [shape(448, 512, dtype=F32)],
        (me, tok, a0, a1, sent, b0, sent_b),
        flops,
        [TOK, *held, dma((1, 2)), dma((6, 2))],
        True,
    )[0]
    sums_a, across_b, own = lax.optimization_barrier((sums_a, across_b, own))
    across_a = lax.all_to_all(sums_a, "y", 0, 0, tiled=True)
    part_b = jnp.sum(across_b.astype(F32), axis=0).astype(BF)
    other_b = swap(part_b, "zl")
    both_b = total(part_b, other_b[::-1]).astype(BF)
    grad_a = jnp.sum(across_a.astype(F32), axis=0).astype(BF)
    more = BACK_CUT - CUT
    first = jnp.concatenate([grad_a, both_b[0, :more]])
    u0, last = lax.optimization_barrier((to_all(first, "y"), both_b[:, more:]))
    v0 = to_all(last, "y")
    u1 = swap(u0, "zl")
    rows = (u0, u1, swap(u0, "c"), swap(u1, "c"), v0, swap(v0, "c"))
    line = call(
        mean_kernel,
        [shape(32, 8, 128, dtype=F32)],
        (me, tok, bend, own, *rows),
        flops,
        [*[ACC] * 3, TOK, *held_back, *map(dma, ((1, 2), (6, 2), (2,)))],
        True,
    )[0]
    whole = jnp.sum(lax.all_to_all(line, REP, 0, 0, tiled=True), axis=0).reshape(2, 512)[:, :448]
    grad = jnp.concatenate([first, last[0]], axis=0).T
    return grad, whole[0], whole[1] / 31


def solution(mesh):
    torus = Mesh(mesh.devices.reshape(8, 2, 2, 4, 4), ("y", "zl", "c", "zh", "x"))
    fsdp = ("zh", "x")
    return jax.shard_map(
        shards,
        mesh=torus,
        in_specs=(P(REP, fsdp),) * 4,
        out_specs=(P(REP, fsdp), P(fsdp), P(fsdp)),
        check_vma=False,
    )
```

```python
import functools

import jax
import jax.numpy as jnp
from jax import lax
from jax.experimental import pallas as pl
from jax.experimental.pallas import tpu as pltpu
from jax.sharding import Mesh
from jax.sharding import PartitionSpec as P

REP = ("y", "zl", "c")
F32, BF = jnp.float32, jnp.bfloat16
NT = (((1,), (1,)), ((), ()))
CUT = 304
VMEM_LIMIT = 60 * 1024 * 1024
TOK = pltpu.VMEM((16, 512, 256), BF)
ACC = pltpu.VMEM((448, 512), F32)
VM = pl.BlockSpec(memory_space=pltpu.VMEM)
ANY = pl.BlockSpec(memory_space=pltpu.HBM)
SM = pl.BlockSpec(memory_space=pltpu.SMEM)


def call(kernel, outs, operands, flops, scratch, near=False):
    moved = sum(a.size * a.dtype.itemsize for a in operands) + sum(
        o.size * o.dtype.itemsize for o in outs
    )
    return pl.pallas_call(
        kernel,
        out_shape=outs,
        in_specs=[SM] + [ANY] * (len(operands) - 1),
        out_specs=[VM if near else ANY] * len(outs),
        scratch_shapes=list(scratch),
        cost_estimate=pl.CostEstimate(flops=flops, bytes_accessed=moved, transcendentals=0),
        compiler_params=pltpu.CompilerParams(vmem_limit_bytes=VMEM_LIMIT),
    )(*operands)


def fetched(pairs, sems):
    def part(i, half):
        source, there = pairs[i]
        count = source.shape[0] // 2
        at = pl.ds(count * half, count)
        return pltpu.make_async_copy(source.at[at], there.at[at], sems.at[i, half])

    for half in (0, 1):
        for i in range(len(pairs)):
            part(i, half).start()

    def ready(half):
        for i in range(len(pairs)):
            part(i, half).wait()

    return ready


def project(me, tok, rows_of, acc, ready):
    mine, first = me[0], me[1] == 0
    for half in (0, 1):
        ready(half)
        rows, cols = [], []
        for y in range(4 * half, 4 * half + 4):
            for rel in (0, 1):
                own, other = rows_of(y, rel)
                rows += [jnp.where(first, own, other), jnp.where(first, other, own)]
                cols.append(tok[2 * y + jnp.bitwise_xor(mine, rel)])
        part = lax.dot_general(
            jnp.concatenate(rows, 1), jnp.concatenate(cols, 1), NT, preferred_element_type=F32
        )
        acc[...] = part if half == 0 else acc[...] + part


def first_kernel(*refs):
    me, t0, p1, p2, m1, m2, f1, f2, up_in, cot_in, *weights = refs[:14]
    tok_out, bend_out, *outs = refs[14:21]
    tok, held, up, cot, coeff, bend, acc, own, own_b, tok_sems, w_sems, in_sems, out_sems, sems = refs[21:]
    mine, first = me[0], me[1] == 0
    sources = ((t0.at[0:2], t0.at[2:4]), (m2, m1), (f1, f2), (p1, p2))

    def token_copy(d, z):
        there = tok.at[4 * z + lax.rem(me[2] + d, 4)]
        return pltpu.make_async_copy(sources[d][z // 2].at[z % 2], there, tok_sems.at[d, z])

    for z in range(4):
        for d in range(4):
            token_copy(d, z).start()
    w_ready = fetched([(w, held.at[i]) for i, w in enumerate(weights)], w_sems)
    get_up = pltpu.make_async_copy(up_in, up, in_sems.at[0])
    get_cot = pltpu.make_async_copy(cot_in, cot, in_sems.at[1])
    get_up.start()
    get_cot.start()

    def ready(half):
        for z in (2 * half, 2 * half + 1):
            for d in range(4):
                token_copy(d, z).wait()
        w_ready(half)

    project(
        me, tok, lambda y, rel: (held[rel, y], held[2 + rel, y]), acc, ready
    )
    keep_tok = pltpu.make_async_copy(tok, tok_out, sems.at[0])
    keep_tok.start()
    get_up.wait()
    get_cot.wait()

    def part(i, unused):
        at = pl.ds(pl.multiple_of(i * 32, 32), 32)
        pre = acc[at, :]
        s = jax.nn.sigmoid(pre)
        one = s * (1.0 + pre * (1.0 - s))
        two = s * (1.0 - s) * (2.0 + pre * (1.0 - 2.0 * s))
        weighted = cot[at, :].astype(F32) * up[at, :].astype(F32)
        coeff[at, :] = (weighted * one).astype(BF)
        bend[at, :] = weighted * two
        return unused

    lax.fori_loop(0, 448 // 32, part, 0)
    keep_bend = pltpu.make_async_copy(bend, bend_out, sems.at[1])
    keep_bend.start()

    def out_copies(i):
        at = pl.ds(2 * i, 2)
        pairs = [(own.at[k, at], outs[k].at[at]) for k in range(2)]
        pairs += [(own.at[2 + k, at], outs[2].at[k, at]) for k in range(2)]
        pairs += [(own_b.at[k, at], outs[3 + k].at[at]) for k in range(2)]
        return [
            pltpu.make_async_copy(here, there, out_sems.at[k, i])
            for k, (here, there) in enumerate(pairs)
        ]

    for i in range(4):
        order = [(y, rel) for y in (2 * i, 2 * i + 1) for rel in (0, 1)]
        tiles = [tok[2 * y + jnp.bitwise_xor(mine, rel)] for y, rel in order]
        got = jnp.dot(
            coeff[...], jnp.concatenate(tiles, 1), preferred_element_type=F32
        ).astype(BF)
        for k, (y, rel) in enumerate(order):
            low, high = got[:, 256 * k : 256 * k + 128], got[:, 256 * k + 128 : 256 * k + 256]
            keep, give = jnp.where(first, low, high), jnp.where(first, high, low)
            own[rel, y] = keep[:CUT]
            own_b[0, y, rel] = keep[CUT:]
            own[2 + rel, y] = give[:CUT]
            own_b[1, y, rel] = give[CUT:]
        for copy in out_copies(i):
            copy.start()
    for i in range(4):
        for copy in out_copies(i):
            copy.wait()
    keep_tok.wait()
    keep_bend.wait()


def both_parts(held, held_b, y, rel):
    return [jnp.concatenate([held[2 * core + rel, y], held_b[core, y, rel]], 0) for core in (0, 1)]


def own_kernel(me, source, a0, a1, sent, b0, b1, acc, tok, held, held_b, tok_sems, sems):
    tok_ready = fetched([(source, tok)], tok_sems)
    pairs = [(a, held.at[i]) for i, a in enumerate((a0, a1, sent.at[0], sent.at[1]))]
    pairs += [(b, held_b.at[i]) for i, b in enumerate((b0, b1))]
    rows_ready = fetched(pairs, sems)

    def ready(half):
        tok_ready(half)
        rows_ready(half)

    project(me, tok, functools.partial(both_parts, held, held_b), acc, ready)


def mean_kernel(me, source, bend_in, own_in, *refs):
    sums, acc, bend, own, tok, held, held_b, tok_sems, sems, in_sems = refs[6:]
    tok_ready = fetched([(source, tok)], tok_sems)
    get_bend = pltpu.make_async_copy(bend_in, bend, in_sems.at[0])
    get_own = pltpu.make_async_copy(own_in, own, in_sems.at[1])
    pairs = [(a, held.at[i]) for i, a in enumerate(refs[:4])]
    pairs += [(b, held_b.at[i]) for i, b in enumerate(refs[4:6])]
    rows_ready = fetched(pairs, sems)
    get_bend.start()
    get_own.start()

    def ready(half):
        tok_ready(half)
        rows_ready(half)

    project(me, tok, functools.partial(both_parts, held, held_b), acc, ready)
    get_bend.wait()
    get_own.wait()
    c = jnp.zeros((448, 128), F32)
    s = jnp.zeros((448, 128), F32)
    for k in range(4):
        lanes = slice(128 * k, 128 * k + 128)
        mean = acc[:, lanes] / 32.0
        b = bend[:, lanes]
        off = own[:, lanes] - mean
        c += b * mean * mean
        s += b * off * off
    for k, terms in enumerate((c, s)):
        line = jnp.sum(terms.T, axis=0, keepdims=True)
        line = jnp.concatenate([line, jnp.zeros((1, 64), F32)], 1)
        for i in range(4):
            row = line[:, 128 * i : 128 * i + 128]
            sums[:, 4 * k + i : 4 * k + i + 1, :] = jnp.broadcast_to(row[None], (32, 1, 128))


def swap(value, axis):
    return lax.ppermute(value, axis, ((0, 1), (1, 0)))


def to_all(value, axis):
    count = lax.axis_size(axis)
    return lax.all_to_all(
        jnp.broadcast_to(value[None], (count, *value.shape)), axis, 0, 0, tiled=True
    )


def total(*values):
    return functools.reduce(jnp.add, [v.astype(F32) for v in values])


def shape(*lengths, dtype=BF):
    return jax.ShapeDtypeStruct(lengths, dtype)


def along_x(value, by):
    return lax.ppermute(value, "x", [(i, (i + by) % 4) for i in range(4)])


def shards(tokens, gate_weight, up_act, cotangent):
    me = jnp.stack([lax.axis_index(axis) for axis in ("zl", "c", "x")]).astype(jnp.int32)
    flops = 2 * 448 * 512 * 4096
    rest = 448 - CUT
    dma = pltpu.SemaphoreType.DMA
    held = [pltpu.VMEM((4, 8, CUT, 128), BF), pltpu.VMEM((2, 8, 2, rest, 128), BF)]
    w0 = lax.all_gather(gate_weight.T, "y", axis=0)
    t0, w0 = lax.optimization_barrier((to_all(tokens, "zh"), w0))
    low, high = t0[:2], t0[2:]
    p1, m1 = along_x(low, 1), along_x(high, -1)
    p2, m2 = along_x(high, 1), along_x(low, -1)
    f1, f2 = along_x(p1, 1), along_x(m1, -1)
    w1, f1, f2 = lax.optimization_barrier((swap(w0, "zl"), f1, f2))
    w0, p2, m2 = lax.optimization_barrier((w0, p2, m2))
    w2, w3 = swap(w0, "c"), swap(w1, "c")
    tok, bend, a0, a1, sent, b0, sent_b = call(
        first_kernel,
        [
            shape(16, 512, 256),
            shape(448, 512, dtype=F32),
            *[shape(8, CUT, 128)] * 2,
            shape(2, 8, CUT, 128),
            *[shape(8, 2, rest, 128)] * 2,
        ],
        (me, t0, p1, p2, m1, m2, f1, f2, up_act.T, cotangent.T, w0, w1, w2, w3),
        2 * flops,
        [
            TOK,
            pltpu.VMEM((4, 8, 448, 128), BF),
            *[pltpu.VMEM((448, 512), BF)] * 3,
            *[ACC] * 2,
            *held,
            *map(dma, ((4, 4), (4, 2), (2,), (6, 4), (2,))),
        ],
    )
    came_b, came = swap(sent_b, "c"), swap(sent, "c")
    sums_b, came = lax.optimization_barrier((total(b0, came_b).astype(BF), came))
    across_b = lax.all_to_all(sums_b, "y", 0, 0, tiled=True)
    came_1 = swap(total(a1, came[1]).astype(BF), "zl")
    sums_a = total(a0, came[0], came_1).astype(BF)
    own = call(
        own_kernel,
        [shape(448, 512, dtype=F32)],
        (me, tok, a0, a1, sent, b0, sent_b),
        flops,
        [TOK, *held, dma((1, 2)), dma((6, 2))],
        True,
    )[0]
    sums_a, across_b, own = lax.optimization_barrier((sums_a, across_b, own))
    across_a = lax.all_to_all(sums_a, "y", 0, 0, tiled=True)
    part_b = jnp.sum(across_b.astype(F32), axis=0).astype(BF)
    other_b = swap(part_b, "zl")
    both_b = total(part_b, other_b[::-1]).astype(BF)
    grad_a = jnp.sum(across_a.astype(F32), axis=0).astype(BF)
    u0, both_b = lax.optimization_barrier((to_all(grad_a, "y"), both_b))
    v0 = to_all(both_b, "y")
    u1 = swap(u0, "zl")
    rows = (u0, u1, swap(u0, "c"), swap(u1, "c"), v0, swap(v0, "c"))
    line = call(
        mean_kernel,
        [shape(32, 8, 128, dtype=F32)],
        (me, tok, bend, own, *rows),
        flops,
        [*[ACC] * 3, TOK, *held, *map(dma, ((1, 2), (6, 2), (2,)))],
        True,
    )[0]
    whole = jnp.sum(lax.all_to_all(line, REP, 0, 0, tiled=True), axis=0).reshape(2, 512)[:, :448]
    grad = jnp.concatenate([grad_a, both_b[0]], axis=0).T
    return grad, whole[0], whole[1] / 31


def solution(mesh):
    torus = Mesh(mesh.devices.reshape(8, 2, 2, 4, 4), ("y", "zl", "c", "zh", "x"))
    fsdp = ("zh", "x")
    return jax.shard_map(
        shards,
        mesh=torus,
        in_specs=(P(REP, fsdp),) * 4,
        out_specs=(P(REP, fsdp), P(fsdp), P(fsdp)),
        check_vma=False,
    )
```

```python
import functools

import jax
import jax.numpy as jnp
from jax import lax
from jax.experimental import pallas as pl
from jax.experimental.pallas import tpu as pltpu
from jax.sharding import Mesh
from jax.sharding import PartitionSpec as P

REP = ("y", "zl", "c")
F32, BF = jnp.float32, jnp.bfloat16
NT = (((1,), (1,)), ((), ()))
CUT = 304
VMEM_LIMIT = 54 * 1024 * 1024
TOK = pltpu.VMEM((16, 512, 256), BF)
ACC = pltpu.VMEM((448, 512), F32)
VM = pl.BlockSpec(memory_space=pltpu.VMEM)
ANY = pl.BlockSpec(memory_space=pltpu.HBM)
SM = pl.BlockSpec(memory_space=pltpu.SMEM)


def call(kernel, outs, operands, flops, scratch, near=False):
    moved = sum(a.size * a.dtype.itemsize for a in operands) + sum(
        o.size * o.dtype.itemsize for o in outs
    )
    return pl.pallas_call(
        kernel,
        out_shape=outs,
        in_specs=[SM] + [ANY] * (len(operands) - 1),
        out_specs=[VM if near else ANY] * len(outs),
        scratch_shapes=list(scratch),
        cost_estimate=pl.CostEstimate(flops=flops, bytes_accessed=moved, transcendentals=0),
        compiler_params=pltpu.CompilerParams(vmem_limit_bytes=VMEM_LIMIT),
    )(*operands)


def fetched(pairs, sems):
    def part(i, half):
        source, there = pairs[i]
        count = source.shape[0] // 2
        at = pl.ds(count * half, count)
        return pltpu.make_async_copy(source.at[at], there.at[at], sems.at[i, half])

    for half in (0, 1):
        for i in range(len(pairs)):
            part(i, half).start()

    def ready(half):
        for i in range(len(pairs)):
            part(i, half).wait()

    return ready


def project(me, tok, rows_of, acc, ready):
    mine, first = me[0], me[1] == 0
    for half in (0, 1):
        ready(half)
        rows, cols = [], []
        for y in range(4 * half, 4 * half + 4):
            for rel in (0, 1):
                own, other = rows_of(y, rel)
                rows += [jnp.where(first, own, other), jnp.where(first, other, own)]
                cols.append(tok[2 * y + jnp.bitwise_xor(mine, rel)])
        part = lax.dot_general(
            jnp.concatenate(rows, 1), jnp.concatenate(cols, 1), NT, preferred_element_type=F32
        )
        acc[...] = part if half == 0 else acc[...] + part


def first_kernel(*refs):
    me, t0, p1, p2, m1, m2, f1, f2, up_in, cot_in, *weights = refs[:14]
    tok_out, bend_out, *outs = refs[14:21]
    tok, held, up, cot, coeff, bend, acc, own, own_b, tok_sems, w_sems, in_sems, out_sems, sems = refs[21:]
    mine, first = me[0], me[1] == 0
    sources = ((t0.at[0:2], t0.at[2:4]), (m2, m1), (f1, f2), (p1, p2))

    def token_copy(d, z):
        there = tok.at[4 * z + lax.rem(me[2] + d, 4)]
        return pltpu.make_async_copy(sources[d][z // 2].at[z % 2], there, tok_sems.at[d, z])

    for z in range(4):
        for d in range(4):
            token_copy(d, z).start()
    w_ready = fetched([(w, held.at[i]) for i, w in enumerate(weights)], w_sems)
    get_up = pltpu.make_async_copy(up_in, up, in_sems.at[0])
    get_cot = pltpu.make_async_copy(cot_in, cot, in_sems.at[1])
    get_up.start()
    get_cot.start()

    def ready(half):
        for z in (2 * half, 2 * half + 1):
            for d in range(4):
                token_copy(d, z).wait()
        w_ready(half)

    project(
        me, tok, lambda y, rel: (held[rel, y], held[2 + rel, y]), acc, ready
    )
    keep_tok = pltpu.make_async_copy(tok, tok_out, sems.at[0])
    keep_tok.start()
    get_up.wait()
    get_cot.wait()

    def part(i, unused):
        at = pl.ds(pl.multiple_of(i * 32, 32), 32)
        pre = acc[at, :]
        s = jax.nn.sigmoid(pre)
        one = s * (1.0 + pre * (1.0 - s))
        two = s * (1.0 - s) * (2.0 + pre * (1.0 - 2.0 * s))
        weighted = cot[at, :].astype(F32) * up[at, :].astype(F32)
        coeff[at, :] = (weighted * one).astype(BF)
        bend[at, :] = weighted * two
        return unused

    lax.fori_loop(0, 448 // 32, part, 0)
    keep_bend = pltpu.make_async_copy(bend, bend_out, sems.at[1])
    keep_bend.start()

    def out_copies(i):
        at = pl.ds(2 * i, 2)
        pairs = [(own.at[k, at], outs[k].at[at]) for k in range(2)]
        pairs += [(own.at[2 + k, at], outs[2].at[k, at]) for k in range(2)]
        pairs += [(own_b.at[k, at], outs[3 + k].at[at]) for k in range(2)]
        return [
            pltpu.make_async_copy(here, there, out_sems.at[k, i])
            for k, (here, there) in enumerate(pairs)
        ]

    for i in range(4):
        order = [(y, rel) for y in (2 * i, 2 * i + 1) for rel in (0, 1)]
        tiles = [tok[2 * y + jnp.bitwise_xor(mine, rel)] for y, rel in order]
        got = jnp.dot(
            coeff[...], jnp.concatenate(tiles, 1), preferred_element_type=F32
        ).astype(BF)
        for k, (y, rel) in enumerate(order):
            low, high = got[:, 256 * k : 256 * k + 128], got[:, 256 * k + 128 : 256 * k + 256]
            keep, give = jnp.where(first, low, high), jnp.where(first, high, low)
            own[rel, y] = keep[:CUT]
            own_b[0, y, rel] = keep[CUT:]
            own[2 + rel, y] = give[:CUT]
            own_b[1, y, rel] = give[CUT:]
        for copy in out_copies(i):
            copy.start()
    for i in range(4):
        for copy in out_copies(i):
            copy.wait()
    keep_tok.wait()
    keep_bend.wait()


def both_parts(held, held_b, y, rel):
    return [jnp.concatenate([held[2 * core + rel, y], held_b[core, y, rel]], 0) for core in (0, 1)]


def own_kernel(me, source, a0, a1, sent, b0, b1, acc, tok, held, held_b, tok_sems, sems):
    tok_ready = fetched([(source, tok)], tok_sems)
    pairs = [(a, held.at[i]) for i, a in enumerate((a0, a1, sent.at[0], sent.at[1]))]
    pairs += [(b, held_b.at[i]) for i, b in enumerate((b0, b1))]
    rows_ready = fetched(pairs, sems)

    def ready(half):
        tok_ready(half)
        rows_ready(half)

    project(me, tok, functools.partial(both_parts, held, held_b), acc, ready)


def mean_kernel(me, source, bend_in, own_in, *refs):
    sums, acc, bend, own, tok, held, held_b, tok_sems, sems, in_sems = refs[6:]
    tok_ready = fetched([(source, tok)], tok_sems)
    get_bend = pltpu.make_async_copy(bend_in, bend, in_sems.at[0])
    get_own = pltpu.make_async_copy(own_in, own, in_sems.at[1])
    pairs = [(a, held.at[i]) for i, a in enumerate(refs[:4])]
    pairs += [(b, held_b.at[i]) for i, b in enumerate(refs[4:6])]
    rows_ready = fetched(pairs, sems)
    get_bend.start()
    get_own.start()

    def ready(half):
        tok_ready(half)
        rows_ready(half)

    project(me, tok, functools.partial(both_parts, held, held_b), acc, ready)
    get_bend.wait()
    get_own.wait()
    c = jnp.zeros((448, 128), F32)
    s = jnp.zeros((448, 128), F32)
    for k in range(4):
        lanes = slice(128 * k, 128 * k + 128)
        mean = acc[:, lanes] / 32.0
        b = bend[:, lanes]
        off = own[:, lanes] - mean
        c += b * mean * mean
        s += b * off * off
    for k, terms in enumerate((c, s)):
        line = jnp.sum(terms.T, axis=0, keepdims=True)
        line = jnp.concatenate([line, jnp.zeros((1, 64), F32)], 1)
        for i in range(4):
            row = line[:, 128 * i : 128 * i + 128]
            sums[:, 4 * k + i : 4 * k + i + 1, :] = jnp.broadcast_to(row[None], (32, 1, 128))


def swap(value, axis):
    return lax.ppermute(value, axis, ((0, 1), (1, 0)))


def to_all(value, axis):
    count = lax.axis_size(axis)
    return lax.all_to_all(
        jnp.broadcast_to(value[None], (count, *value.shape)), axis, 0, 0, tiled=True
    )


def total(*values):
    return functools.reduce(jnp.add, [v.astype(F32) for v in values])


def shape(*lengths, dtype=BF):
    return jax.ShapeDtypeStruct(lengths, dtype)


def along_x(value, by):
    return lax.ppermute(value, "x", [(i, (i + by) % 4) for i in range(4)])


def shards(tokens, gate_weight, up_act, cotangent):
    me = jnp.stack([lax.axis_index(axis) for axis in ("zl", "c", "x")]).astype(jnp.int32)
    flops = 2 * 448 * 512 * 4096
    rest = 448 - CUT
    dma = pltpu.SemaphoreType.DMA
    held = [pltpu.VMEM((4, 8, CUT, 128), BF), pltpu.VMEM((2, 8, 2, rest, 128), BF)]
    w0 = lax.all_gather(gate_weight.T, "y", axis=0)
    t0, w0 = lax.optimization_barrier((to_all(tokens, "zh"), w0))
    low, high = t0[:2], t0[2:]
    p1, m1 = along_x(low, 1), along_x(high, -1)
    p2, m2 = along_x(high, 1), along_x(low, -1)
    f1, f2 = along_x(p1, 1), along_x(m1, -1)
    w1, f1, f2 = lax.optimization_barrier((swap(w0, "zl"), f1, f2))
    w0, p2, m2 = lax.optimization_barrier((w0, p2, m2))
    w2, w3 = swap(w0, "c"), swap(w1, "c")
    tok, bend, a0, a1, sent, b0, sent_b = call(
        first_kernel,
        [
            shape(16, 512, 256),
            shape(448, 512, dtype=F32),
            *[shape(8, CUT, 128)] * 2,
            shape(2, 8, CUT, 128),
            *[shape(8, 2, rest, 128)] * 2,
        ],
        (me, t0, p1, p2, m1, m2, f1, f2, up_act.T, cotangent.T, w0, w1, w2, w3),
        2 * flops,
        [
            TOK,
            pltpu.VMEM((4, 8, 448, 128), BF),
            *[pltpu.VMEM((448, 512), BF)] * 3,
            *[ACC] * 2,
            *held,
            *map(dma, ((4, 4), (4, 2), (2,), (6, 4), (2,))),
        ],
    )
    came_b, came = swap(sent_b, "c"), swap(sent, "c")
    sums_b, came = lax.optimization_barrier((total(b0, came_b).astype(BF), came))
    across_b = lax.all_to_all(sums_b, "y", 0, 0, tiled=True)
    came_1 = swap(total(a1, came[1]).astype(BF), "zl")
    sums_a = total(a0, came[0], came_1).astype(BF)
    own = call(
        own_kernel,
        [shape(448, 512, dtype=F32)],
        (me, tok, a0, a1, sent, b0, sent_b),
        flops,
        [TOK, *held, dma((1, 2)), dma((6, 2))],
        True,
    )[0]
    sums_a, across_b, own = lax.optimization_barrier((sums_a, across_b, own))
    across_a = lax.all_to_all(sums_a, "y", 0, 0, tiled=True)
    part_b = jnp.sum(across_b.astype(F32), axis=0).astype(BF)
    other_b = swap(part_b, "zl")
    both_b = total(part_b, other_b[::-1]).astype(BF)
    grad_a = jnp.sum(across_a.astype(F32), axis=0).astype(BF)
    u0, both_b = lax.optimization_barrier((to_all(grad_a, "y"), both_b))
    v0 = to_all(both_b, "y")
    u1 = swap(u0, "zl")
    rows = (u0, u1, swap(u0, "c"), swap(u1, "c"), v0, swap(v0, "c"))
    line = call(
        mean_kernel,
        [shape(32, 8, 128, dtype=F32)],
        (me, tok, bend, own, *rows),
        flops,
        [*[ACC] * 3, TOK, *held, *map(dma, ((1, 2), (6, 2), (2,)))],
        True,
    )[0]
    whole = jnp.sum(lax.all_to_all(line, REP, 0, 0, tiled=True), axis=0).reshape(2, 512)[:, :448]
    grad = jnp.concatenate([grad_a, both_b[0]], axis=0).T
    return grad, whole[0], whole[1] / 31


def solution(mesh):
    torus = Mesh(mesh.devices.reshape(8, 2, 2, 4, 4), ("y", "zl", "c", "zh", "x"))
    fsdp = ("zh", "x")
    return jax.shard_map(
        shards,
        mesh=torus,
        in_specs=(P(REP, fsdp),) * 4,
        out_specs=(P(REP, fsdp), P(fsdp), P(fsdp)),
        check_vma=False,
    )
```

```python
import functools

import jax
import jax.numpy as jnp
from jax import lax
from jax.experimental import pallas as pl
from jax.experimental.pallas import tpu as pltpu
from jax.sharding import Mesh
from jax.sharding import PartitionSpec as P

REP = ("y", "zl", "c")
F32, BF = jnp.float32, jnp.bfloat16
NT = (((1,), (1,)), ((), ()))
CUT = 304
VMEM_LIMIT = 54 * 1024 * 1024
TOK = pltpu.VMEM((16, 512, 256), BF)
ACC = pltpu.VMEM((448, 512), F32)
VM = pl.BlockSpec(memory_space=pltpu.VMEM)
ANY = pl.BlockSpec(memory_space=pltpu.HBM)
SM = pl.BlockSpec(memory_space=pltpu.SMEM)


def call(kernel, outs, operands, flops, scratch, near=False):
    moved = sum(a.size * a.dtype.itemsize for a in operands) + sum(
        o.size * o.dtype.itemsize for o in outs
    )
    return pl.pallas_call(
        kernel,
        out_shape=outs,
        in_specs=[SM] + [ANY] * (len(operands) - 1),
        out_specs=[VM if near else ANY] * len(outs),
        scratch_shapes=list(scratch),
        cost_estimate=pl.CostEstimate(flops=flops, bytes_accessed=moved, transcendentals=0),
        compiler_params=pltpu.CompilerParams(vmem_limit_bytes=VMEM_LIMIT),
    )(*operands)


def fetched(pairs, sems):
    def part(i, half):
        source, there = pairs[i]
        count = source.shape[0] // 2
        at = pl.ds(count * half, count)
        return pltpu.make_async_copy(source.at[at], there.at[at], sems.at[i, half])

    for half in (0, 1):
        for i in range(len(pairs)):
            part(i, half).start()

    def ready(half):
        for i in range(len(pairs)):
            part(i, half).wait()

    return ready


def project(me, tok, rows_of, acc, ready):
    mine, first = me[0], me[1] == 0
    for half in (0, 1):
        ready(half)
        rows, cols = [], []
        for y in range(4 * half, 4 * half + 4):
            for rel in (0, 1):
                own, other = rows_of(y, rel)
                rows += [jnp.where(first, own, other), jnp.where(first, other, own)]
                cols.append(tok[2 * y + jnp.bitwise_xor(mine, rel)])
        part = lax.dot_general(
            jnp.concatenate(rows, 1), jnp.concatenate(cols, 1), NT, preferred_element_type=F32
        )
        acc[...] = part if half == 0 else acc[...] + part


def first_kernel(*refs):
    me, t0, p1, p2, m1, m2, f1, f2, up_in, cot_in, *weights = refs[:14]
    tok_out, bend_out, *outs = refs[14:21]
    tok, held, up, cot, coeff, bend, acc, own, own_b, tok_sems, w_sems, in_sems, out_sems, sems = refs[21:]
    mine, first = me[0], me[1] == 0
    sources = ((t0.at[0:2], t0.at[2:4]), (m2, m1), (f1, f2), (p1, p2))

    def token_copy(d, z):
        there = tok.at[4 * z + lax.rem(me[2] + d, 4)]
        return pltpu.make_async_copy(sources[d][z // 2].at[z % 2], there, tok_sems.at[d, z])

    for z in range(4):
        for d in range(4):
            token_copy(d, z).start()
    w_ready = fetched([(w, held.at[i]) for i, w in enumerate(weights)], w_sems)
    get_up = pltpu.make_async_copy(up_in, up, in_sems.at[0])
    get_cot = pltpu.make_async_copy(cot_in, cot, in_sems.at[1])
    get_up.start()
    get_cot.start()

    def ready(half):
        for z in (2 * half, 2 * half + 1):
            for d in range(4):
                token_copy(d, z).wait()
        w_ready(half)

    project(
        me, tok, lambda y, rel: (held[rel, y], held[2 + rel, y]), acc, ready
    )
    keep_tok = pltpu.make_async_copy(tok, tok_out, sems.at[0])
    keep_tok.start()
    get_up.wait()
    get_cot.wait()

    def part(i, unused):
        at = pl.ds(pl.multiple_of(i * 32, 32), 32)
        pre = acc[at, :]
        s = jax.nn.sigmoid(pre)
        one = s * (1.0 + pre * (1.0 - s))
        two = s * (1.0 - s) * (2.0 + pre * (1.0 - 2.0 * s))
        weighted = cot[at, :].astype(F32) * up[at, :].astype(F32)
        coeff[at, :] = (weighted * one).astype(BF)
        bend[at, :] = weighted * two
        return unused

    lax.fori_loop(0, 448 // 32, part, 0)
    keep_bend = pltpu.make_async_copy(bend, bend_out, sems.at[1])
    keep_bend.start()

    def out_copies(i):
        at = pl.ds(2 * i, 2)
        pairs = [(own.at[k, at], outs[k].at[at]) for k in range(2)]
        pairs += [(own.at[2 + k, at], outs[2].at[k, at]) for k in range(2)]
        pairs += [(own_b.at[k, at], outs[3 + k].at[at]) for k in range(2)]
        return [
            pltpu.make_async_copy(here, there, out_sems.at[k, i])
            for k, (here, there) in enumerate(pairs)
        ]

    for i in range(4):
        order = [(y, rel) for y in (2 * i, 2 * i + 1) for rel in (0, 1)]
        tiles = [tok[2 * y + jnp.bitwise_xor(mine, rel)] for y, rel in order]
        got = jnp.dot(
            coeff[...], jnp.concatenate(tiles, 1), preferred_element_type=F32
        ).astype(BF)
        for k, (y, rel) in enumerate(order):
            low, high = got[:, 256 * k : 256 * k + 128], got[:, 256 * k + 128 : 256 * k + 256]
            keep, give = jnp.where(first, low, high), jnp.where(first, high, low)
            own[rel, y] = keep[:CUT]
            own_b[0, y, rel] = keep[CUT:]
            own[2 + rel, y] = give[:CUT]
            own_b[1, y, rel] = give[CUT:]
        for copy in out_copies(i):
            copy.start()
    for i in range(4):
        for copy in out_copies(i):
            copy.wait()
    keep_tok.wait()
    keep_bend.wait()


def both_parts(held, held_b, y, rel):
    return [jnp.concatenate([held[2 * core + rel, y], held_b[core, y, rel]], 0) for core in (0, 1)]


def own_kernel(me, source, a0, a1, sent, b0, b1, acc, tok, held, held_b, tok_sems, sems):
    tok_ready = fetched([(source, tok)], tok_sems)
    pairs = [(a, held.at[i]) for i, a in enumerate((a0, a1, sent.at[0], sent.at[1]))]
    pairs += [(b, held_b.at[i]) for i, b in enumerate((b0, b1))]
    rows_ready = fetched(pairs, sems)

    def ready(half):
        tok_ready(half)
        rows_ready(half)

    project(me, tok, functools.partial(both_parts, held, held_b), acc, ready)


def mean_kernel(me, source, bend_in, own_in, *refs):
    sums, acc, bend, own, tok, held, held_b, tok_sems, sems, in_sems = refs[6:]
    tok_ready = fetched([(source, tok)], tok_sems)
    get_bend = pltpu.make_async_copy(bend_in, bend, in_sems.at[0])
    get_own = pltpu.make_async_copy(own_in, own, in_sems.at[1])
    pairs = [(a, held.at[i]) for i, a in enumerate(refs[:4])]
    pairs += [(b, held_b.at[i]) for i, b in enumerate(refs[4:6])]
    rows_ready = fetched(pairs, sems)
    get_bend.start()
    get_own.start()

    def ready(half):
        tok_ready(half)
        rows_ready(half)

    project(me, tok, functools.partial(both_parts, held, held_b), acc, ready)
    get_bend.wait()
    get_own.wait()
    c = jnp.zeros((448, 128), F32)
    s = jnp.zeros((448, 128), F32)
    for k in range(4):
        lanes = slice(128 * k, 128 * k + 128)
        mean = acc[:, lanes] / 32.0
        b = bend[:, lanes]
        off = own[:, lanes] - mean
        c += b * mean * mean
        s += b * off * off
    for k, terms in enumerate((c, s)):
        line = jnp.sum(terms.T, axis=0, keepdims=True)
        line = jnp.concatenate([line, jnp.zeros((1, 64), F32)], 1)
        for i in range(4):
            row = line[:, 128 * i : 128 * i + 128]
            sums[:, 4 * k + i : 4 * k + i + 1, :] = jnp.broadcast_to(row[None], (32, 1, 128))


def swap(value, axis):
    return lax.ppermute(value, axis, ((0, 1), (1, 0)))


def to_all(value, axis):
    count = lax.axis_size(axis)
    return lax.all_to_all(
        jnp.broadcast_to(value[None], (count, *value.shape)), axis, 0, 0, tiled=True
    )


def total(*values):
    return functools.reduce(jnp.add, [v.astype(F32) for v in values])


def shape(*lengths, dtype=BF):
    return jax.ShapeDtypeStruct(lengths, dtype)


def along_x(value, by):
    return lax.ppermute(value, "x", [(i, (i + by) % 4) for i in range(4)])


def shards(tokens, gate_weight, up_act, cotangent):
    me = jnp.stack([lax.axis_index(axis) for axis in ("zl", "c", "x")]).astype(jnp.int32)
    flops = 2 * 448 * 512 * 4096
    rest = 448 - CUT
    dma = pltpu.SemaphoreType.DMA
    held = [pltpu.VMEM((4, 8, CUT, 128), BF), pltpu.VMEM((2, 8, 2, rest, 128), BF)]
    w0 = lax.all_gather(gate_weight.T, "y", axis=0)
    t0, w0 = lax.optimization_barrier((to_all(tokens, "zh"), w0))
    low, high = t0[:2], t0[2:]
    p1, m1 = along_x(low, 1), along_x(high, -1)
    p2, m2 = along_x(high, 1), along_x(low, -1)
    f1, f2 = along_x(p1, 1), along_x(m1, -1)
    w1, f1, f2 = lax.optimization_barrier((swap(w0, "zl"), f1, f2))
    w0, p2, m2 = lax.optimization_barrier((w0, p2, m2))
    w2, w3 = swap(w0, "c"), swap(w1, "c")
    tok, bend, a0, a1, sent, b0, sent_b = call(
        first_kernel,
        [
            shape(16, 512, 256),
            shape(448, 512, dtype=F32),
            *[shape(8, CUT, 128)] * 2,
            shape(2, 8, CUT, 128),
            *[shape(8, 2, rest, 128)] * 2,
        ],
        (me, t0, p1, p2, m1, m2, f1, f2, up_act.T, cotangent.T, w0, w1, w2, w3),
        2 * flops,
        [
            TOK,
            pltpu.VMEM((4, 8, 448, 128), BF),
            *[pltpu.VMEM((448, 512), BF)] * 3,
            *[ACC] * 2,
            *held,
            *map(dma, ((4, 4), (4, 2), (2,), (6, 4), (2,))),
        ],
    )
    came_b, came = swap(sent_b, "c"), swap(sent, "c")
    sums_b, came = lax.optimization_barrier((total(b0, came_b).astype(BF), came))
    across_b = lax.all_to_all(sums_b, "y", 0, 0, tiled=True)
    came_1 = swap(total(a1, came[1]).astype(BF), "zl")
    sums_a = total(a0, came[0], came_1).astype(BF)
    own = call(
        own_kernel,
        [shape(448, 512, dtype=F32)],
        (me, tok, a0, a1, sent, b0, sent_b),
        flops,
        [TOK, *held, dma((1, 2)), dma((6, 2))],
        True,
    )[0]
    sums_a, across_b, own = lax.optimization_barrier((sums_a, across_b, own))
    across_a = lax.all_to_all(sums_a, "y", 0, 0, tiled=True)
    part_b = jnp.sum(across_b.astype(F32), axis=0).astype(BF)
    other_b = swap(part_b, "zl")
    both_b = total(part_b, other_b[::-1]).astype(BF)
    grad_a = jnp.sum(across_a.astype(F32), axis=0).astype(BF)
    u0, both_b = lax.optimization_barrier((to_all(grad_a, "y"), both_b))
    v0 = to_all(both_b, "y")
    u1 = swap(u0, "zl")
    v1 = swap(v0, "c")
    u1, v1 = lax.optimization_barrier((u1, v1))
    rows = (u0, u1, swap(u0, "c"), swap(u1, "c"), v0, v1)
    line = call(
        mean_kernel,
        [shape(32, 8, 128, dtype=F32)],
        (me, tok, bend, own, *rows),
        flops,
        [*[ACC] * 3, TOK, *held, *map(dma, ((1, 2), (6, 2), (2,)))],
        True,
    )[0]
    whole = jnp.sum(lax.all_to_all(line, REP, 0, 0, tiled=True), axis=0).reshape(2, 512)[:, :448]
    grad = jnp.concatenate([grad_a, both_b[0]], axis=0).T
    return grad, whole[0], whole[1] / 31


def solution(mesh):
    torus = Mesh(mesh.devices.reshape(8, 2, 2, 4, 4), ("y", "zl", "c", "zh", "x"))
    fsdp = ("zh", "x")
    return jax.shard_map(
        shards,
        mesh=torus,
        in_specs=(P(REP, fsdp),) * 4,
        out_specs=(P(REP, fsdp), P(fsdp), P(fsdp)),
        check_vma=False,
    )
```
